256 devices in a mesh: dp: 16 (over x_hi, z), tensor: 16 (over x_lo, y, core).
Axes of the slice: x: 4 (x_hi: 2, x_lo: 2; x = x_hi * 2 + x_lo), y: 4, z: 8, core: 2. Of those that a mesh axis runs over, the one named last changes fastest.
Arguments:
- final_layer_states: bfloat16 [32768, 8192], P('dp', 'tensor'), may hold values from -64 to 64
- entry_rms_multiplier: float32 [8192], replicated, may hold values from 0.25 to 1.75
- group_sharpness: float32 [64], replicated, may hold values from 0.1 to 1
- ancestor_ids: int32 [32768], P('dp'), may hold values from 0 to 62, as said below
- proposal_matrix: bfloat16 [8192, 4096], P('dp', 'tensor'), may hold values from -0.0625 to 0.0625
- future_vectors: bfloat16 [32768, 4096], P('dp', 'tensor'), may hold values from -6 to 6
Outputs:
- predicted: bfloat16 [32768, 4096], P('dp', 'tensor')
- weight_grad: float32 [8192, 4096], P('dp', 'tensor')
The draws below stay inside these ranges and needn't reach their ends.
Inputs may be any that keep to these rules, and one draw needn't show every extreme that they name: `ancestor_ids`: within each aligned block of 64 tokens, a token's entry is the in-block index of its parent, smaller than its own in-block index; the block's first token has 0, and its last token's parent is the one just before it.
All inputs are finite; a program needn't handle non-finite values.
Results may differ from the reference program's by a relative error of at most 0.012.
Values may be sent and summed in bfloat16 or wider, within the bound.
No kernel may reach another device: no remote copies, remote signals or barrier semaphores. Data moves between devices by JAX's collectives and lax.ppermute only.
A program may use at most 128 MiB of HBM per device.

```python
import math
import jax
import jax.numpy as jnp
from jax import lax

D = 8192
QUERY_GROUP_TOTAL = 64
PER_GROUP_DEPTH = 128
DOUT = 4096
BLOCK = 64
TOKENS = 32768


def draw_ancestor_ids(key, part):
    position = jnp.arange(TOKENS, dtype=jnp.int32) % BLOCK
    drawn_ints = jax.random.randint(key, (TOKENS,), 0, BLOCK, dtype=jnp.int32)
    chosen = drawn_ints % jnp.maximum(position, 1)
    return jnp.where(position == BLOCK - 1, position - 1, chosen).astype(jnp.int32)


def draw_final_layer_states(key, part):
    keys = jax.random.split(key, 3)
    position = jnp.arange(TOKENS, dtype=jnp.int32) % BLOCK
    blocks = TOKENS // BLOCK
    block_head = jax.random.randint(keys[1], (blocks,), 0, QUERY_GROUP_TOTAL, dtype=jnp.int32)
    block_amp = jax.random.uniform(keys[2], (blocks,), jnp.float32, 5.0, 9.0)
    token_head = jnp.repeat(block_head, BLOCK)
    token_amp = jnp.repeat(block_amp, BLOCK)
    feature_head = jnp.arange(D, dtype=jnp.int32) // PER_GROUP_DEPTH
    base = jnp.clip(jax.random.normal(keys[0], (TOKENS, D), jnp.float32), -6.0, 6.0)
    drawn = base
    earlier = jnp.roll(base, 1, axis=0)
    child = (position == BLOCK - 1)[:, None]
    special = (position >= BLOCK - 2)[:, None]
    in_head = feature_head[None, :] == token_head[:, None]
    focused = jnp.where(child, earlier + 0.15 * base, base) * token_amp[:, None]
    row = jnp.where(special, jnp.where(in_head, focused, 0.1 * base), drawn)
    return jnp.clip(row, -64.0, 64.0).astype(jnp.bfloat16)


def steps_of(key, extent, cuts, least, largest):
    def one(dim, shards_of):
        draws = jax.random.uniform(jax.random.fold_in(jax.random.fold_in(key, 6), dim), (shards_of,), jnp.float32, least / len(cuts), largest / len(cuts))
        return jnp.repeat(jnp.exp(draws), extent[dim] // shards_of).reshape((-1,) + (1,) * (len(extent) - dim - 1))

    gain = one(*cuts[0])
    for cut in cuts[1:]:
        gain = gain * one(*cut)
    return gain


def noise(stream_key, extent, scale, bound, pieces=(), kind=jnp.bfloat16):
    drawn = scale * jax.random.normal(stream_key, extent, jnp.float32)
    if pieces:
        drawn = drawn * steps_of(stream_key, extent, pieces, -0.22, 0.18)
    return jnp.clip(drawn, -bound, bound).astype(kind)


def setup_inputs(seed: int = 0) -> dict:
    seeds = jax.random.split(jax.random.key(seed), 7)
    final_layer_states = draw_final_layer_states(jax.random.fold_in(seeds[6], 71), 0)
    entry_rms_multiplier = jnp.clip(1.0 + 0.15 * jax.random.normal(seeds[1], (D,), jnp.float32), 0.25, 1.75)
    group_sharpness = jnp.clip(jnp.exp(jax.random.uniform(seeds[2], (QUERY_GROUP_TOTAL,), jnp.float32, math.log(0.1), math.log(1.0))), 0.1, 1.0)
    ancestor_ids = draw_ancestor_ids(jax.random.fold_in(seeds[6], 71), 0)
    proposal_matrix = noise(seeds[4], (D, DOUT), D ** -0.5, 0.0625, ((0, 16), (1, 16)))
    future_vectors = noise(seeds[5], (TOKENS, DOUT), 1.0, 6.0, ((0, 16), (1, 16)))
    return {"final_layer_states": final_layer_states, "entry_rms_multiplier": entry_rms_multiplier, "group_sharpness": group_sharpness, "ancestor_ids": ancestor_ids, "proposal_matrix": proposal_matrix, "future_vectors": future_vectors}


def tree_reach(ancestor_ids):
    blocks = ancestor_ids.shape[0] // BLOCK
    index = jnp.arange(BLOCK, dtype=jnp.int32)
    grouped = ancestor_ids.reshape(blocks, BLOCK).astype(jnp.int32)
    link = ((grouped[:, :, None] == index[None, None, :]) & (index[None, :, None] > 0)).astype(jnp.float32)
    reach = link + jnp.eye(BLOCK, dtype=jnp.float32)[None]
    for sweep in range(6):
        reach = jnp.minimum(jnp.einsum('bts,bsu->btu', reach, reach, precision=lax.Precision.HIGHEST), 1.0)
    return reach

def branching_query_mixer(rescaled_entry, ancestor_ids, group_sharpness):
    rows = rescaled_entry.shape[0]
    blocks = rows // BLOCK
    reach = tree_reach(ancestor_ids)
    feats = rescaled_entry.reshape(blocks, BLOCK, QUERY_GROUP_TOTAL, PER_GROUP_DEPTH).astype(jnp.float32)
    softmax_multiplier = group_sharpness.astype(jnp.float32) / math.sqrt(PER_GROUP_DEPTH)
    scores = jnp.einsum('bthd,bshd->bhts', feats, feats) * softmax_multiplier[None, :, None, None]
    scores = jnp.where(reach[:, None] > 0, scores, -1e+30)
    top = lax.optimization_barrier(jnp.max(scores, axis=-1, keepdims=True))
    expd = jnp.exp(scores - top)
    probs = (expd / lax.optimization_barrier(jnp.sum(expd, axis=-1, keepdims=True))).astype(jnp.bfloat16)
    blended_result = jnp.einsum('bhts,bshd->bthd', probs.astype(jnp.float32), feats)
    return blended_result.astype(jnp.bfloat16).reshape(rows, QUERY_GROUP_TOTAL * PER_GROUP_DEPTH)

def reference(final_layer_states, entry_rms_multiplier, group_sharpness, ancestor_ids, proposal_matrix, future_vectors):
    wide_rows = final_layer_states.astype(jnp.float32)
    mean_sq = lax.optimization_barrier(jnp.mean(wide_rows * wide_rows, axis=1, keepdims=True))
    rescaled_entry = (wide_rows * lax.rsqrt(mean_sq + 1e-05) * entry_rms_multiplier[None, :]).astype(jnp.bfloat16)
    blended_result = branching_query_mixer(rescaled_entry, ancestor_ids, group_sharpness)
    projected = jnp.dot(blended_result, proposal_matrix, preferred_element_type=jnp.float32)
    predicted = projected.astype(jnp.bfloat16)
    residual_grad = jnp.clip(projected - future_vectors.astype(jnp.float32), -1.0, 1.0).astype(jnp.bfloat16)
    weight_grad = lax.dot_general(blended_result, residual_grad, (((0,), (0,)), ((), ())), preferred_element_type=jnp.float32)
    return (predicted, weight_grad / math.sqrt(TOKENS))
```

```python
import functools
import math

import jax
import jax.numpy as jnp
from jax import lax
from jax.experimental import pallas as pl
from jax.experimental.pallas import tpu as pltpu
from jax.sharding import Mesh
from jax.sharding import PartitionSpec as P

HEAD = 128
BLOCK = 64
GROUP = 128
EPS = 1e-05
CHUNKS = (2048,)
BF16 = jnp.bfloat16
F32 = jnp.float32

GATHER_A = ((0, 2), (1, 0), (2, 3), (3, 1))
GATHER_B = ((1, 2), (2, 1))
SCATTER_A = tuple((dst, src) for src, dst in GATHER_A)
SCATTER_B = GATHER_B


def ring(n, step):
    return [(i, (i + step) % n) for i in range(n)]


def params(mib=48):
    return pltpu.CompilerParams(vmem_limit_bytes=mib * 1024 * 1024)


def reach_kernel(ids_ref, bias_ref):
    groups = ids_ref.shape[0]
    row = lax.broadcasted_iota(jnp.int32, (GROUP, GROUP), 0)
    col = lax.broadcasted_iota(jnp.int32, (GROUP, GROUP), 1)
    base = jnp.where(col >= BLOCK, BLOCK, 0)
    inner = (col != 0) & (col != BLOCK)
    eye = row == col
    reach = []
    for g in range(groups):
        parent = ids_ref[g : g + 1, :] + base
        hit = ((parent == row) & inner) | eye
        reach.append(jnp.where(hit, 1.0, 0.0).astype(BF16))
    for sweep in range(6):
        reach = [
            jnp.minimum(jnp.dot(r, r, preferred_element_type=F32), 1.0).astype(BF16) for r in reach
        ]
    for g in range(groups):
        bias = jnp.where(reach[g].astype(F32) > 0.0, 0.0, -1e30)
        bias_ref[g * GROUP : (g + 1) * GROUP, :] = bias.T


def reach_bias(ids):
    groups = ids.shape[0]
    return pl.pallas_call(
        reach_kernel,
        out_shape=jax.ShapeDtypeStruct((groups * GROUP, GROUP), F32),
        compiler_params=params(16),
        cost_estimate=pl.CostEstimate(
            flops=groups * 6 * 2 * GROUP**3, bytes_accessed=groups * GROUP * GROUP * 4, transcendentals=0
        ),
        name="reach",
    )(ids)


def attention_kernel(width, x_ref, sq_ref, bias_ref, gain_ref, sharp_ref, out_ref):
    groups = x_ref.shape[0] // GROUP
    heads = x_ref.shape[1] // HEAD
    row = lax.broadcasted_iota(jnp.int32, (GROUP, GROUP), 0)
    col = lax.broadcasted_iota(jnp.int32, (GROUP, GROUP), 1)
    eye = row == col
    gain = gain_ref[...]
    for g in range(groups):
        rows = slice(g * GROUP, (g + 1) * GROUP)
        scale = lax.rsqrt(sq_ref[0, g : g + 1, :] * (1.0 / width) + EPS)
        scale = jnp.sum(jnp.where(eye, scale, 0.0), axis=1, keepdims=True)
        normed = (x_ref[rows, :].astype(F32) * scale * gain).astype(BF16)
        bias = bias_ref[rows, :]
        for h in range(heads):
            cols = slice(h * HEAD, (h + 1) * HEAD)
            feats = normed[:, cols]
            scores = lax.dot_general(
                feats, feats, (((1,), (1,)), ((), ())), preferred_element_type=F32
            )
            scores = scores * (sharp_ref[0, h] * (1.0 / math.sqrt(HEAD))) + bias
            top = jnp.max(scores, axis=1, keepdims=True)
            expd = jnp.exp(scores - top)
            probs = (expd / jnp.sum(expd, axis=1, keepdims=True)).astype(BF16)
            mixed = jnp.dot(probs, feats, preferred_element_type=F32)
            out_ref[rows, cols] = mixed.astype(BF16)


def attention(states, squares, bias, gain, sharp, width, start, rows):
    cols = states.shape[1]
    tile = min(rows, 256)
    first = start // tile
    sub = tile // GROUP
    return pl.pallas_call(
        functools.partial(attention_kernel, width),
        grid=(rows // tile,),
        in_specs=[
            pl.BlockSpec((tile, cols), lambda i: (first + i, 0)),
            pl.BlockSpec((1, sub, GROUP), lambda i: (first + i, 0, 0)),
            pl.BlockSpec((tile, GROUP), lambda i: (first + i, 0)),
            pl.BlockSpec((1, cols), lambda i: (0, 0)),
            pl.BlockSpec(memory_space=pltpu.SMEM),
        ],
        out_specs=pl.BlockSpec((tile, cols), lambda i: (i, 0)),
        out_shape=jax.ShapeDtypeStruct((rows, cols), BF16),
        compiler_params=params(16),
        cost_estimate=pl.CostEstimate(
            flops=rows * GROUP * cols * 16, bytes_accessed=rows * cols * 4, transcendentals=rows * GROUP * 4
        ),
        name="attention",
    )(states, squares.reshape(-1, sub, GROUP), bias, gain, sharp)


def forward_kernel(pos_ref, mixed_ref, keep_w_ref, send_w_ref, keep_ref, send_ref):
    blocks = mixed_ref.shape[0]
    mixed = jnp.concatenate([mixed_ref[b] for b in range(blocks)], axis=1)
    depth = mixed.shape[1]
    keep_ref[...] = jnp.dot(
        mixed, keep_w_ref[...].reshape(depth, -1), preferred_element_type=F32
    )
    send_ref[...] = jnp.dot(
        mixed, send_w_ref[...].reshape(depth, -1), preferred_element_type=F32
    ).astype(BF16)


def forward(pos, mixed, weight):
    blocks, rows, depth = mixed.shape
    cols = weight.shape[3]
    tile = min(rows, 256)
    grid_spec = pltpu.PrefetchScalarGridSpec(
        num_scalar_prefetch=1,
        grid=(rows // tile,),
        in_specs=[
            pl.BlockSpec((blocks, tile, depth), lambda i, pos: (0, i, 0)),
            pl.BlockSpec((blocks, None, depth, cols), lambda i, pos: (0, pos[0], 0, 0)),
            pl.BlockSpec((blocks, None, depth, cols), lambda i, pos: (0, 1 - pos[0], 0, 0)),
        ],
        out_specs=[
            pl.BlockSpec((tile, cols), lambda i, pos: (i, 0)),
            pl.BlockSpec((tile, cols), lambda i, pos: (i, 0)),
        ],
    )
    return pl.pallas_call(
        forward_kernel,
        grid_spec=grid_spec,
        out_shape=[
            jax.ShapeDtypeStruct((rows, cols), F32),
            jax.ShapeDtypeStruct((rows, cols), BF16),
        ],
        compiler_params=params(),
        cost_estimate=pl.CostEstimate(
            flops=4 * rows * blocks * depth * cols,
            bytes_accessed=2 * rows * blocks * depth + 4 * blocks * depth * cols,
            transcendentals=0,
        ),
        name="forward",
    )(pos, mixed, weight, weight)


def gradient_kernel(steps, has_acc, mixed_ref, left_ref, right_ref, *refs):
    if has_acc:
        acc_in, out_ref, acc_ref = refs
    else:
        acc_in = None
        out_ref, acc_ref = refs
    step = pl.program_id(0)
    half = left_ref.shape[1]
    blocks = mixed_ref.shape[0]
    grads = (left_ref[...].astype(F32).T.astype(BF16), right_ref[...].astype(F32).T.astype(BF16))

    def term(b, s):
        return jnp.dot(grads[s], mixed_ref[b], preferred_element_type=F32)

    @pl.when(step == 0)
    def _():
        for b in range(blocks):
            for s in range(2):
                rows = slice(s * half, (s + 1) * half)
                value = term(b, s)
                if has_acc:
                    value = value + acc_in[b, rows, :]
                acc_ref[b, rows, :] = value

    @pl.when(step > 0)
    def _():
        for b in range(blocks):
            for s in range(2):
                rows = slice(s * half, (s + 1) * half)
                acc_ref[b, rows, :] += term(b, s)

    @pl.when(step == steps - 1)
    def _():
        out_ref[...] = acc_ref[...].astype(out_ref.dtype)


def gradient(mixed, left, right, acc, dtype):
    blocks, rows, depth = mixed.shape
    half = left.shape[1]
    tile = min(rows, 256)
    steps = rows // tile
    shape = (blocks, 2 * half, depth)
    whole = pl.BlockSpec(shape, lambda i: (0, 0, 0), pipeline_mode=pl.Buffered(1))
    in_specs = [
        pl.BlockSpec((blocks, tile, depth), lambda i: (0, i, 0)),
        pl.BlockSpec((tile, half), lambda i: (i, 0)),
        pl.BlockSpec((tile, half), lambda i: (i, 0)),
    ]
    operands = [mixed, left, right]
    if acc is not None:
        in_specs.append(whole)
        operands.append(acc)
    return pl.pallas_call(
        functools.partial(gradient_kernel, steps, acc is not None),
        grid=(steps,),
        in_specs=in_specs,
        out_specs=whole,
        out_shape=jax.ShapeDtypeStruct(shape, dtype),
        scratch_shapes=[pltpu.VMEM(shape, F32)],
        compiler_params=params(),
        cost_estimate=pl.CostEstimate(
            flops=4 * rows * blocks * depth * half,
            bytes_accessed=2 * rows * blocks * depth + 4 * blocks * depth * half,
            transcendentals=0,
        ),
        name="gradient",
    )(*operands)


def tensor_sum(value):
    value = value + sum(lax.ppermute(value, "y", ring(4, k)) for k in (1, 2, 3))
    value = value + lax.ppermute(value, "xl", ring(2, 1))
    return value + lax.ppermute(value, "c", ring(2, 1))


def body(states, gain, sharpness, ancestor_ids, proposal, future):
    tokens, width = states.shape
    total_width = gain.shape[0]
    xh, xl = lax.axis_index("xh"), lax.axis_index("xl")
    place = lax.axis_index(("xl", "y", "c"))
    heads = width // HEAD
    out_cols = proposal.shape[1]

    first = lax.ppermute(proposal, ("xh", "xl"), GATHER_A)
    second = lax.ppermute(proposal, ("xh", "xl"), GATHER_B)
    second = jnp.where(xh == xl, proposal, second)
    left_first = xh == 1
    pair = jnp.stack([jnp.where(left_first, first, second), jnp.where(left_first, second, first)])
    weight = lax.all_gather(pair, "z", axis=0, tiled=False)

    wide = states.astype(F32)
    squares = tensor_sum(jnp.sum(wide * wide, axis=1).reshape(-1, GROUP))
    bias = reach_bias(ancestor_ids.reshape(-1, GROUP))
    my_gain = lax.dynamic_slice_in_dim(gain, place * width, width).reshape(1, width)
    my_sharp = lax.dynamic_slice_in_dim(sharpness, place * heads, heads).reshape(1, heads)
    pos = xl.astype(jnp.int32).reshape(1)

    predicted = []
    start = 0
    acc = None
    for index, rows in enumerate(CHUNKS):
        mixed = attention(states, squares, bias, my_gain, my_sharp, total_width, start, rows)
        mixed = lax.all_gather(mixed, ("y", "c"), axis=0, tiled=False)
        keep, send = forward(pos, mixed, weight)
        result = keep + lax.ppermute(send, "xl", ring(2, 1)).astype(F32)
        predicted.append(result.astype(BF16))
        target = lax.slice_in_dim(future, start, start + rows).astype(F32)
        mine = jnp.clip(result - target, -1.0, 1.0).astype(BF16)
        other = lax.ppermute(mine, "xl", ring(2, 1))
        left = jnp.where(xl == 0, mine, other)
        right = jnp.where(xl == 0, other, mine)
        last = index == len(CHUNKS) - 1
        acc = gradient(mixed, left, right, acc, BF16 if last else F32)
        start += rows

    summed = lax.psum_scatter(acc, "z", scatter_dimension=0, tiled=False)
    low, high = summed[:out_cols], summed[out_cols:]
    to_a = jnp.where(xh == 1, low, high)
    to_b = jnp.where(xh == 1, high, low)
    got_a = lax.ppermute(to_a, ("xh", "xl"), SCATTER_A)
    got_b = lax.ppermute(to_b, ("xh", "xl"), SCATTER_B)
    got_b = jnp.where(xh == xl, to_b, got_b)
    weight_grad = (got_a.astype(F32) + got_b.astype(F32)).T / math.sqrt(
        tokens * lax.axis_size("xh") * lax.axis_size("z")
    )
    return jnp.concatenate(predicted), weight_grad


def solution(mesh):
    grid = Mesh(mesh.devices.reshape(2, 8, 2, 4, 2), ("xh", "z", "xl", "y", "c"))
    dp, tensor = ("xh", "z"), ("xl", "y", "c")
    return jax.shard_map(
        body,
        mesh=grid,
        in_specs=(P(dp, tensor), P(), P(), P(dp), P(dp, tensor), P(dp, tensor)),
        out_specs=(P(dp, tensor), P(dp, tensor)),
        check_vma=False,
    )
```

```python
import functools
import math

import jax
import jax.numpy as jnp
from jax import lax
from jax.experimental import pallas as pl
from jax.experimental.pallas import tpu as pltpu
from jax.sharding import Mesh
from jax.sharding import PartitionSpec as P

HEAD = 128
BLOCK = 64
GROUP = 128
EPS = 1e-05
CHUNKS = (512, 512, 512, 512)
BF16 = jnp.bfloat16
F32 = jnp.float32

GATHER_A = ((0, 2), (1, 0), (2, 3), (3, 1))
GATHER_B = ((1, 2), (2, 1))
SCATTER_A = tuple((dst, src) for src, dst in GATHER_A)
SCATTER_B = GATHER_B


def ring(n, step):
    return [(i, (i + step) % n) for i in range(n)]


def params(mib=48):
    return pltpu.CompilerParams(vmem_limit_bytes=mib * 1024 * 1024)


def reach_kernel(ids_ref, bias_ref):
    groups = ids_ref.shape[0]
    row = lax.broadcasted_iota(jnp.int32, (GROUP, GROUP), 0)
    col = lax.broadcasted_iota(jnp.int32, (GROUP, GROUP), 1)
    base = jnp.where(col >= BLOCK, BLOCK, 0)
    inner = (col != 0) & (col != BLOCK)
    eye = row == col
    reach = []
    for g in range(groups):
        parent = ids_ref[g : g + 1, :] + base
        hit = ((parent == row) & inner) | eye
        reach.append(jnp.where(hit, 1.0, 0.0).astype(BF16))
    for sweep in range(6):
        reach = [
            jnp.minimum(jnp.dot(r, r, preferred_element_type=F32), 1.0).astype(BF16) for r in reach
        ]
    for g in range(groups):
        bias = jnp.where(reach[g].astype(F32) > 0.0, 0.0, -1e30)
        bias_ref[g * GROUP : (g + 1) * GROUP, :] = bias.T


def reach_bias(ids):
    groups = ids.shape[0]
    return pl.pallas_call(
        reach_kernel,
        out_shape=jax.ShapeDtypeStruct((groups * GROUP, GROUP), F32),
        compiler_params=params(16),
        cost_estimate=pl.CostEstimate(
            flops=groups * 6 * 2 * GROUP**3, bytes_accessed=groups * GROUP * GROUP * 4, transcendentals=0
        ),
        name="reach",
    )(ids)


def attention_kernel(width, x_ref, sq_ref, bias_ref, gain_ref, sharp_ref, out_ref):
    groups = x_ref.shape[0] // GROUP
    heads = x_ref.shape[1] // HEAD
    row = lax.broadcasted_iota(jnp.int32, (GROUP, GROUP), 0)
    col = lax.broadcasted_iota(jnp.int32, (GROUP, GROUP), 1)
    eye = row == col
    gain = gain_ref[...]
    ones = jnp.ones((GROUP, HEAD), BF16)
    where = [
        (slice(g * GROUP, (g + 1) * GROUP), slice(h * HEAD, (h + 1) * HEAD), h)
        for g in range(groups)
        for h in range(heads)
    ]
    feats = []
    for g in range(groups):
        rows = slice(g * GROUP, (g + 1) * GROUP)
        scale = lax.rsqrt(sq_ref[0, g : g + 1, :] * (1.0 / width) + EPS)
        scale = jnp.sum(jnp.where(eye, scale, 0.0), axis=1, keepdims=True)
        normed = (x_ref[rows, :].astype(F32) * scale * gain).astype(BF16)
        feats += [normed[:, h * HEAD : (h + 1) * HEAD] for h in range(heads)]
    factor = math.log2(math.e) / math.sqrt(HEAD)
    scores = [
        lax.dot_general(f, f, (((1,), (1,)), ((), ())), preferred_element_type=F32) for f in feats
    ]
    scores = [
        s * (sharp_ref[0, h] * factor) + bias_ref[rows, :] for s, (rows, _, h) in zip(scores, where)
    ]
    tops = [jnp.max(s, axis=1, keepdims=True) for s in scores]
    terms = [jnp.exp2(s - top).astype(BF16) for s, top in zip(scores, tops)]
    sums = [
        jnp.dot(t, jnp.concatenate([f, ones], axis=1), preferred_element_type=F32)
        for t, f in zip(terms, feats)
    ]
    for value, (rows, cols, _) in zip(sums, where):
        out_ref[rows, cols] = (value[:, :HEAD] / value[:, HEAD:]).astype(BF16)


def attention(states, squares, bias, gain, sharp, width, start, rows):
    cols = states.shape[1]
    tile = min(rows, 256)
    first = start // tile
    sub = tile // GROUP
    return pl.pallas_call(
        functools.partial(attention_kernel, width),
        grid=(rows // tile,),
        in_specs=[
            pl.BlockSpec((tile, cols), lambda i: (first + i, 0)),
            pl.BlockSpec((1, sub, GROUP), lambda i: (first + i, 0, 0)),
            pl.BlockSpec((tile, GROUP), lambda i: (first + i, 0)),
            pl.BlockSpec((1, cols), lambda i: (0, 0)),
            pl.BlockSpec(memory_space=pltpu.SMEM),
        ],
        out_specs=pl.BlockSpec((tile, cols), lambda i: (i, 0)),
        out_shape=jax.ShapeDtypeStruct((rows, cols), BF16),
        compiler_params=params(16),
        cost_estimate=pl.CostEstimate(
            flops=rows * GROUP * cols * 16, bytes_accessed=rows * cols * 4, transcendentals=rows * GROUP * 4
        ),
        name="attention",
    )(states, squares.reshape(-1, sub, GROUP), bias, gain, sharp)


def forward_kernel(pos_ref, *refs):
    mixed, (keep_w_ref, send_w_ref, keep_ref, send_ref) = refs[:-4], refs[-4:]

    def product(weight_ref):
        total = None
        for b, ref in enumerate(mixed):
            term = jnp.dot(ref[...], weight_ref[pos_ref[1 + b]], preferred_element_type=F32)
            total = term if total is None else total + term
        return total

    send_ref[...] = product(send_w_ref).astype(BF16)
    keep_ref[...] = product(keep_w_ref)


def forward(pos, mixed, weight):
    blocks, _, depth, cols = weight.shape
    rows = mixed[0].shape[0]
    tile = min(rows, 256)
    grid_spec = pltpu.PrefetchScalarGridSpec(
        num_scalar_prefetch=1,
        grid=(rows // tile,),
        in_specs=[pl.BlockSpec((tile, depth), lambda i, pos: (i, 0)) for _ in mixed]
        + [
            pl.BlockSpec((blocks, None, depth, cols), lambda i, pos: (0, pos[0], 0, 0)),
            pl.BlockSpec((blocks, None, depth, cols), lambda i, pos: (0, 1 - pos[0], 0, 0)),
        ],
        out_specs=[
            pl.BlockSpec((tile, cols), lambda i, pos: (i, 0)),
            pl.BlockSpec((tile, cols), lambda i, pos: (i, 0)),
        ],
    )
    return pl.pallas_call(
        forward_kernel,
        grid_spec=grid_spec,
        out_shape=[
            jax.ShapeDtypeStruct((rows, cols), F32),
            jax.ShapeDtypeStruct((rows, cols), BF16),
        ],
        compiler_params=params(24),
        cost_estimate=pl.CostEstimate(
            flops=4 * rows * blocks * depth * cols,
            bytes_accessed=2 * rows * blocks * depth + 4 * blocks * depth * cols,
            transcendentals=0,
        ),
        name="forward",
    )(pos, *mixed, weight, weight)


def gradient_kernel(steps, has_acc, pos_ref, *refs):
    refs = list(refs)
    acc_ref = refs.pop()
    out_ref = refs.pop()
    acc_in = refs.pop() if has_acc else None
    other_ref = refs.pop()
    mine_ref = refs.pop()
    step = pl.program_id(0)
    grads = (
        (pos_ref[0], mine_ref[...].astype(F32).T.astype(BF16)),
        (1 - pos_ref[0], other_ref[...].astype(F32).T.astype(BF16)),
    )

    def sweep(base, target):
        for b, ref in enumerate(refs):
            place = pos_ref[1 + b]
            for half, grad in grads:
                value = jnp.dot(grad, ref[...], preferred_element_type=F32)
                if base is not None:
                    value = value + base[place, half]
                target[place, half] = value.astype(target.dtype)

    if steps == 1:
        sweep(acc_in, out_ref)
        return

    @pl.when(step == 0)
    def _():
        sweep(acc_in, acc_ref)

    if steps > 2:

        @pl.when((step > 0) & (step < steps - 1))
        def _():
            sweep(acc_ref, acc_ref)

    @pl.when(step == steps - 1)
    def _():
        sweep(acc_ref, out_ref)


def gradient(pos, mixed, mine, other, acc, dtype):
    blocks = len(mixed)
    rows, depth = mixed[0].shape
    half = mine.shape[1]
    tile = min(rows, 512)
    steps = rows // tile
    shape = (blocks, 2, half, depth)
    whole = pl.BlockSpec(shape, lambda i, pos: (0, 0, 0, 0), pipeline_mode=pl.Buffered(1))
    in_specs = [pl.BlockSpec((tile, depth), lambda i, pos: (i, 0)) for _ in mixed]
    in_specs += [pl.BlockSpec((tile, half), lambda i, pos: (i, 0))] * 2
    operands = [*mixed, mine, other]
    if acc is not None:
        in_specs.append(whole)
        operands.append(acc)
    return pl.pallas_call(
        functools.partial(gradient_kernel, steps, acc is not None),
        grid_spec=pltpu.PrefetchScalarGridSpec(
            num_scalar_prefetch=1,
            grid=(steps,),
            in_specs=in_specs,
            out_specs=whole,
            scratch_shapes=[pltpu.VMEM(shape if steps > 1 else (8, 128), F32)],
        ),
        out_shape=jax.ShapeDtypeStruct(shape, dtype),
        compiler_params=params(40),
        cost_estimate=pl.CostEstimate(
            flops=4 * rows * blocks * depth * half,
            bytes_accessed=2 * rows * blocks * depth + 8 * blocks * depth * half,
            transcendentals=0,
        ),
        name="gradient",
    )(pos, *operands)


def gather(mixed, index):
    up = lax.ppermute(mixed, "y", ring(4, 1))
    down = lax.ppermute(mixed, "y", ring(4, -1))
    far = lax.ppermute(up if index % 2 == 0 else down, "y", ring(4, 1 if index % 2 == 0 else -1))
    here = (mixed, up, down, far)
    return (*here, *(lax.ppermute(value, "c", ring(2, 1)) for value in here))


def tensor_sum(value):
    value = value + lax.ppermute(value, "c", ring(2, 1))
    value = value + sum(lax.ppermute(value, "y", ring(4, k)) for k in (1, 2, 3))
    return value + lax.ppermute(value, "xl", ring(2, 1))


def body(states, gain, sharpness, ancestor_ids, proposal, future):
    tokens, width = states.shape
    total_width = gain.shape[0]
    xh, xl = lax.axis_index("xh"), lax.axis_index("xl")
    place = lax.axis_index(("xl", "y", "c"))
    heads = width // HEAD

    first = lax.ppermute(proposal, ("xh", "xl"), GATHER_A)
    second = lax.ppermute(proposal, ("xh", "xl"), GATHER_B)
    second = jnp.where(xh == xl, proposal, second)
    left_first = xh == 1
    pair = jnp.stack([jnp.where(left_first, first, second), jnp.where(left_first, second, first)])
    weight = lax.all_gather(pair, "z", axis=0, tiled=False)

    wide = states.astype(F32)
    squares = tensor_sum(jnp.sum(wide * wide, axis=1).reshape(-1, GROUP))
    bias = reach_bias(ancestor_ids.reshape(-1, GROUP))
    my_gain = lax.dynamic_slice_in_dim(gain, place * width, width).reshape(1, width)
    my_sharp = lax.dynamic_slice_in_dim(sharpness, place * heads, heads).reshape(1, heads)
    y, c = lax.axis_index("y"), lax.axis_index("c")
    order = [2 * ((y + dy) % 4) + (c + dc) % 2 for dc in (0, 1) for dy in (0, 3, 1, 2)]
    pos = jnp.stack([xl, *order]).astype(jnp.int32)

    predicted = []
    start = 0
    acc = None
    for index, rows in enumerate(CHUNKS):
        mixed = attention(states, squares, bias, my_gain, my_sharp, total_width, start, rows)
        mixed = gather(mixed, index)
        keep, send = forward(pos, mixed, weight)
        result = keep + lax.ppermute(send, "xl", ring(2, 1)).astype(F32)
        predicted.append(result.astype(BF16))
        target = lax.slice_in_dim(future, start, start + rows).astype(F32)
        mine = jnp.clip(result - target, -1.0, 1.0).astype(BF16)
        other = lax.ppermute(mine, "xl", ring(2, 1))
        last = index == len(CHUNKS) - 1
        acc = gradient(pos, mixed, mine, other, acc, BF16 if last else F32)
        start += rows

    summed = lax.psum_scatter(acc, "z", scatter_dimension=0, tiled=False)
    low, high = summed[0], summed[1]
    to_a = jnp.where(xh == 1, low, high)
    to_b = jnp.where(xh == 1, high, low)
    got_a = lax.ppermute(to_a, ("xh", "xl"), SCATTER_A)
    got_b = lax.ppermute(to_b, ("xh", "xl"), SCATTER_B)
    got_b = jnp.where(xh == xl, to_b, got_b)
    weight_grad = (got_a.astype(F32) + got_b.astype(F32)).T / math.sqrt(
        tokens * lax.axis_size("xh") * lax.axis_size("z")
    )
    return jnp.concatenate(predicted), weight_grad


def solution(mesh):
    grid = Mesh(mesh.devices.reshape(2, 8, 2, 4, 2), ("xh", "z", "xl", "y", "c"))
    dp, tensor = ("xh", "z"), ("xl", "y", "c")
    return jax.shard_map(
        body,
        mesh=grid,
        in_specs=(P(dp, tensor), P(), P(), P(dp), P(dp, tensor), P(dp, tensor)),
        out_specs=(P(dp, tensor), P(dp, tensor)),
        check_vma=False,
    )
```

```python
import functools
import math

import jax
import jax.numpy as jnp
from jax import lax
from jax.experimental import pallas as pl
from jax.experimental.pallas import tpu as pltpu
from jax.sharding import Mesh
from jax.sharding import PartitionSpec as P

HEAD = 128
BLOCK = 64
GROUP = 128
EPS = 1e-05
CHUNKS = (512, 512, 512, 512)
BF16 = jnp.bfloat16
F32 = jnp.float32

GATHER_A = ((0, 2), (1, 0), (2, 3), (3, 1))
GATHER_B = ((1, 2), (2, 1))
SCATTER_A = tuple((dst, src) for src, dst in GATHER_A)
SCATTER_B = GATHER_B


def ring(n, step):
    return [(i, (i + step) % n) for i in range(n)]


def params(mib=48):
    return pltpu.CompilerParams(vmem_limit_bytes=mib * 1024 * 1024)


def reach_kernel(ids_ref, bias_ref):
    groups = ids_ref.shape[0]
    row = lax.broadcasted_iota(jnp.int32, (GROUP, GROUP), 0)
    col = lax.broadcasted_iota(jnp.int32, (GROUP, GROUP), 1)
    base = jnp.where(col >= BLOCK, BLOCK, 0)
    inner = (col != 0) & (col != BLOCK)
    eye = row == col
    reach = []
    for g in range(groups):
        parent = ids_ref[g : g + 1, :] + base
        hit = ((parent == row) & inner) | eye
        reach.append(jnp.where(hit, 1.0, 0.0).astype(BF16))
    for sweep in range(6):
        reach = [
            jnp.minimum(jnp.dot(r, r, preferred_element_type=F32), 1.0).astype(BF16) for r in reach
        ]
    for g in range(groups):
        bias = jnp.where(reach[g].astype(F32) > 0.0, 0.0, -1e30)
        bias_ref[g * GROUP : (g + 1) * GROUP, :] = bias.T


def reach_bias(ids):
    groups = ids.shape[0]
    return pl.pallas_call(
        reach_kernel,
        out_shape=jax.ShapeDtypeStruct((groups * GROUP, GROUP), F32),
        compiler_params=params(16),
        cost_estimate=pl.CostEstimate(
            flops=groups * 6 * 2 * GROUP**3, bytes_accessed=groups * GROUP * GROUP * 4, transcendentals=0
        ),
        name="reach",
    )(ids)


def attention_kernel(width, x_ref, sq_ref, bias_ref, gain_ref, sharp_ref, out_ref):
    groups = x_ref.shape[0] // GROUP
    heads = x_ref.shape[1] // HEAD
    row = lax.broadcasted_iota(jnp.int32, (GROUP, GROUP), 0)
    col = lax.broadcasted_iota(jnp.int32, (GROUP, GROUP), 1)
    eye = row == col
    gain = gain_ref[...]
    ones = jnp.ones((GROUP, HEAD), BF16)
    where = [
        (slice(g * GROUP, (g + 1) * GROUP), slice(h * HEAD, (h + 1) * HEAD), h)
        for g in range(groups)
        for h in range(heads)
    ]
    feats = []
    for g in range(groups):
        rows = slice(g * GROUP, (g + 1) * GROUP)
        scale = lax.rsqrt(sq_ref[0, g : g + 1, :] * (1.0 / width) + EPS)
        scale = jnp.sum(jnp.where(eye, scale, 0.0), axis=1, keepdims=True)
        normed = (x_ref[rows, :].astype(F32) * scale * gain).astype(BF16)
        feats += [normed[:, h * HEAD : (h + 1) * HEAD] for h in range(heads)]
    factor = math.log2(math.e) / math.sqrt(HEAD)
    scores = [
        lax.dot_general(f, f, (((1,), (1,)), ((), ())), preferred_element_type=F32) for f in feats
    ]
    scores = [
        s * (sharp_ref[0, h] * factor) + bias_ref[rows, :] for s, (rows, _, h) in zip(scores, where)
    ]
    tops = [jnp.max(s, axis=1, keepdims=True) for s in scores]
    terms = [jnp.exp2(s - top).astype(BF16) for s, top in zip(scores, tops)]
    sums = [
        jnp.dot(t, jnp.concatenate([f, ones], axis=1), preferred_element_type=F32)
        for t, f in zip(terms, feats)
    ]
    for value, (rows, cols, _) in zip(sums, where):
        out_ref[rows, cols] = (value[:, :HEAD] / value[:, HEAD:]).astype(BF16)


def attention(states, squares, bias, gain, sharp, width, start, rows):
    cols = states.shape[1]
    tile = min(rows, 256)
    first = start // tile
    sub = tile // GROUP
    return pl.pallas_call(
        functools.partial(attention_kernel, width),
        grid=(rows // tile,),
        in_specs=[
            pl.BlockSpec((tile, cols), lambda i: (first + i, 0)),
            pl.BlockSpec((1, sub, GROUP), lambda i: (first + i, 0, 0)),
            pl.BlockSpec((tile, GROUP), lambda i: (first + i, 0)),
            pl.BlockSpec((1, cols), lambda i: (0, 0)),
            pl.BlockSpec(memory_space=pltpu.SMEM),
        ],
        out_specs=pl.BlockSpec((tile, cols), lambda i: (i, 0)),
        out_shape=jax.ShapeDtypeStruct((rows, cols), BF16),
        compiler_params=params(16),
        cost_estimate=pl.CostEstimate(
            flops=rows * GROUP * cols * 16, bytes_accessed=rows * cols * 4, transcendentals=rows * GROUP * 4
        ),
        name="attention",
    )(states, squares.reshape(-1, sub, GROUP), bias, gain, sharp)


def forward_kernel(pos_ref, *refs):
    mixed, (weight_ref, keep_ref, send_ref) = refs[:-3], refs[-3:]

    def product(half):
        total = None
        for b, ref in enumerate(mixed):
            term = jnp.dot(ref[...], weight_ref[pos_ref[1 + b], half], preferred_element_type=F32)
            total = term if total is None else total + term
        return total

    send_ref[...] = product(1 - pos_ref[0]).astype(BF16)
    keep_ref[...] = product(pos_ref[0])


def vmem():
    return pl.BlockSpec(memory_space=pltpu.VMEM)


def smem():
    return pl.BlockSpec(memory_space=pltpu.SMEM)


def forward(pos, mixed, weight):
    blocks, _, depth, cols = weight.shape
    rows = mixed[0].shape[0]
    return pl.pallas_call(
        forward_kernel,
        in_specs=[smem()] + [vmem()] * (len(mixed) + 1),
        out_specs=[vmem()] * 2,
        out_shape=[
            jax.ShapeDtypeStruct((rows, cols), F32),
            jax.ShapeDtypeStruct((rows, cols), BF16),
        ],
        compiler_params=params(24),
        cost_estimate=pl.CostEstimate(
            flops=4 * rows * blocks * depth * cols,
            bytes_accessed=2 * rows * blocks * depth + 4 * blocks * depth * cols,
            transcendentals=0,
        ),
        name="forward",
    )(pos, *mixed, weight)


def gradient_kernel(chunks, has_acc, pos_ref, *refs):
    refs = list(refs)
    out_ref = refs.pop()
    acc_ref = refs.pop() if has_acc else None
    blocks = len(refs) // chunks - 2
    mixed = [refs[n * blocks : (n + 1) * blocks] for n in range(chunks)]
    grads = refs[chunks * blocks :]
    grads = [g[...].astype(F32).T.astype(BF16) for g in grads]
    halves = ((pos_ref[0], grads[:chunks]), (1 - pos_ref[0], grads[chunks:]))
    for b in range(blocks):
        place = pos_ref[1 + b]
        for half, grad in halves:
            value = acc_ref[place, half] if has_acc else None
            for n in range(chunks):
                term = jnp.dot(grad[n], mixed[n][b][...], preferred_element_type=F32)
                value = term if value is None else value + term
            out_ref[place, half] = value.astype(out_ref.dtype)


def gradient(pos, mixed, mine, other, acc, dtype):
    blocks = len(mixed[0])
    rows = sum(m[0].shape[0] for m in mixed)
    depth = mixed[0][0].shape[1]
    half = mine[0].shape[1]
    operands = [*(value for chunk in mixed for value in chunk), *mine, *other]
    if acc is not None:
        operands.append(acc)
    return pl.pallas_call(
        functools.partial(gradient_kernel, len(mixed), acc is not None),
        in_specs=[smem()] + [vmem()] * len(operands),
        out_specs=vmem(),
        out_shape=jax.ShapeDtypeStruct((blocks, 2, half, depth), dtype),
        compiler_params=params(40),
        cost_estimate=pl.CostEstimate(
            flops=4 * rows * blocks * depth * half,
            bytes_accessed=2 * rows * blocks * depth + 8 * blocks * depth * half,
            transcendentals=0,
        ),
        name="gradient",
    )(pos, *operands)


def after(value, *others):
    return lax.optimization_barrier((value, *others))[0]


def swap(value, axis):
    return lax.ppermute(value, axis, ring(2, 1))


def body(states, gain, sharpness, ancestor_ids, proposal, future):
    tokens, width = states.shape
    total_width = gain.shape[0]
    xh, xl = lax.axis_index("xh"), lax.axis_index("xl")
    y, c = lax.axis_index("y"), lax.axis_index("c")
    heads = width // HEAD

    order = [2 * ((y + dy) & 3) + (c ^ dc) for dc in (0, 1) for dy in (0, 3, 1, 2)]
    pos = jnp.stack([xl, *order]).astype(jnp.int32)
    place = 8 * xl + 2 * y + c
    my_gain = lax.dynamic_slice_in_dim(gain, place * width, width).reshape(1, width)
    my_sharp = lax.dynamic_slice_in_dim(sharpness, place * heads, heads).reshape(1, heads)
    bias = reach_bias(ancestor_ids.reshape(-1, GROUP))

    wide = states.astype(F32)
    squares = jnp.sum(wide * wide, axis=1).reshape(-1, GROUP)
    squares = squares + swap(squares, "c")
    squares = squares + swap(squares, "xl")
    proposal = after(proposal, squares)
    first = lax.ppermute(proposal, ("xh", "xl"), GATHER_A)
    second = lax.ppermute(proposal, ("xh", "xl"), GATHER_B)
    squares = squares + sum(lax.ppermute(squares, "y", ring(4, k)) for k in (1, 2, 3))

    count = len(CHUNKS)
    starts = [sum(CHUNKS[:i]) for i in range(count)]
    mixed = [
        attention(states, squares, bias, my_gain, my_sharp, total_width, start, rows)
        for start, rows in zip(starts, CHUNKS)
    ]
    first, second = after((first, second), mixed[0])
    second = jnp.where(xh == xl, proposal, second)
    pair = jnp.stack([jnp.where(xh == 1, first, second), jnp.where(xh == 1, second, first)])
    weight = lax.all_gather(pair, "z", axis=0, tiled=False)

    predicted, full, keep, send, mine, other = [], [], [], [], [], []

    def receive(i):
        result = keep[i] + swap(send[i], "xl").astype(F32)
        predicted.append(result.astype(BF16))
        target = lax.slice_in_dim(future, starts[i], starts[i] + CHUNKS[i]).astype(F32)
        mine.append(jnp.clip(result - target, -1.0, 1.0).astype(BF16))
        other.append(swap(mine[i], "xl"))

    def multiply(i):
        kept, sent = forward(pos, full[i], weight)
        keep.append(kept)
        send.append(sent)

    acc = None
    up = down = None
    for i in range(count):
        source = mixed[i]
        if i > 0:
            source = after(source, up, down)
        if i == count - 1:
            multiply(0)
            source = after(source, send[0])
        up = lax.ppermute(source, "y", ring(4, 1))
        down = lax.ppermute(source, "y", ring(4, -1))
        relay = up if i % 2 == 0 else down
        if i == count - 1:
            multiply(1)
            relay = after(relay, send[1])
        far = lax.ppermute(relay, "y", ring(4, 1 if i % 2 == 0 else -1))
        if i == count - 1:
            receive(0)
            full[2] = [after(full[2][0], mine[0]), *full[2][1:]]
            multiply(2)
            receive(1)
            far = after(far, send[2], mine[1])
        here = (source, up, down, far)
        full.append([*here, *(swap(value, "c") for value in here)])
    acc = gradient(pos, full[:2], mine[:2], other[:2], None, F32)
    receive(2)
    full[3] = [after(full[3][0], acc, mine[2]), *full[3][1:]]
    multiply(3)
    receive(3)
    acc = gradient(pos, full[2:], mine[2:], other[2:], acc, BF16)

    summed = lax.psum_scatter(acc, "z", scatter_dimension=0, tiled=False)
    low, high = summed[0], summed[1]
    to_a = jnp.where(xh == 1, low, high)
    to_b = jnp.where(xh == 1, high, low)
    got_a = lax.ppermute(to_a, ("xh", "xl"), SCATTER_A)
    got_b = lax.ppermute(to_b, ("xh", "xl"), SCATTER_B)
    got_b = jnp.where(xh == xl, to_b, got_b)
    weight_grad = (got_a.astype(F32) + got_b.astype(F32)).T / math.sqrt(
        tokens * lax.axis_size("xh") * lax.axis_size("z")
    )
    return jnp.concatenate(predicted), weight_grad


def solution(mesh):
    grid = Mesh(mesh.devices.reshape(2, 8, 2, 4, 2), ("xh", "z", "xl", "y", "c"))
    dp, tensor = ("xh", "z"), ("xl", "y", "c")
    return jax.shard_map(
        body,
        mesh=grid,
        in_specs=(P(dp, tensor), P(), P(), P(dp), P(dp, tensor), P(dp, tensor)),
        out_specs=(P(dp, tensor), P(dp, tensor)),
        check_vma=False,
    )
```

```python
import functools
import math

import jax
import jax.numpy as jnp
from jax import lax
from jax.experimental import pallas as pl
from jax.experimental.pallas import tpu as pltpu
from jax.sharding import Mesh
from jax.sharding import PartitionSpec as P

HEAD = 128
BLOCK = 64
GROUP = 128
EPS = 1e-05
CHUNKS = (512, 512, 512, 512)
FAR = (True, False, True, False)
BF16 = jnp.bfloat16
F32 = jnp.float32

GATHER_A = ((0, 2), (1, 0), (2, 3), (3, 1))
GATHER_B = ((1, 2), (2, 1))
SCATTER_A = tuple((dst, src) for src, dst in GATHER_A)
SCATTER_B = GATHER_B


def ring(n, step):
    return [(i, (i + step) % n) for i in range(n)]


def params(mib=48):
    return pltpu.CompilerParams(vmem_limit_bytes=mib * 1024 * 1024)


def reach_kernel(ids_ref, bias_ref):
    groups = ids_ref.shape[0]
    row = lax.broadcasted_iota(jnp.int32, (GROUP, GROUP), 0)
    col = lax.broadcasted_iota(jnp.int32, (GROUP, GROUP), 1)
    base = jnp.where(col >= BLOCK, BLOCK, 0)
    inner = (col != 0) & (col != BLOCK)
    eye = row == col
    reach = []
    for g in range(groups):
        parent = ids_ref[g : g + 1, :] + base
        hit = ((parent == row) & inner) | eye
        reach.append(jnp.where(hit, 1.0, 0.0).astype(BF16))
    for sweep in range(6):
        reach = [
            jnp.minimum(jnp.dot(r, r, preferred_element_type=F32), 1.0).astype(BF16) for r in reach
        ]
    for g in range(groups):
        bias = jnp.where(reach[g].astype(F32) > 0.0, 0.0, -1e30)
        bias_ref[g * GROUP : (g + 1) * GROUP, :] = bias.T


def reach_bias(ids):
    groups = ids.shape[0]
    return pl.pallas_call(
        reach_kernel,
        out_shape=jax.ShapeDtypeStruct((groups * GROUP, GROUP), F32),
        compiler_params=params(16),
        cost_estimate=pl.CostEstimate(
            flops=groups * 6 * 2 * GROUP**3, bytes_accessed=groups * GROUP * GROUP * 4, transcendentals=0
        ),
        name="reach",
    )(ids)


def attention_kernel(width, x_ref, sq_ref, bias_ref, gain_ref, sharp_ref, out_ref):
    groups = x_ref.shape[0] // GROUP
    heads = x_ref.shape[1] // HEAD
    row = lax.broadcasted_iota(jnp.int32, (GROUP, GROUP), 0)
    col = lax.broadcasted_iota(jnp.int32, (GROUP, GROUP), 1)
    eye = row == col
    gain = gain_ref[...]
    ones = jnp.ones((GROUP, HEAD), BF16)
    where = [
        (slice(g * GROUP, (g + 1) * GROUP), slice(h * HEAD, (h + 1) * HEAD), h)
        for g in range(groups)
        for h in range(heads)
    ]
    feats = []
    for g in range(groups):
        rows = slice(g * GROUP, (g + 1) * GROUP)
        scale = lax.rsqrt(sq_ref[0, g : g + 1, :] * (1.0 / width) + EPS)
        scale = jnp.sum(jnp.where(eye, scale, 0.0), axis=1, keepdims=True)
        normed = (x_ref[rows, :].astype(F32) * scale * gain).astype(BF16)
        feats += [normed[:, h * HEAD : (h + 1) * HEAD] for h in range(heads)]
    factor = math.log2(math.e) / math.sqrt(HEAD)
    scores = [
        lax.dot_general(f, f, (((1,), (1,)), ((), ())), preferred_element_type=F32) for f in feats
    ]
    scores = [
        s * (sharp_ref[0, h] * factor) + bias_ref[rows, :] for s, (rows, _, h) in zip(scores, where)
    ]
    tops = [jnp.max(s, axis=1, keepdims=True) for s in scores]
    terms = [jnp.exp2(s - top).astype(BF16) for s, top in zip(scores, tops)]
    sums = [
        jnp.dot(t, jnp.concatenate([f, ones], axis=1), preferred_element_type=F32)
        for t, f in zip(terms, feats)
    ]
    for value, (rows, cols, _) in zip(sums, where):
        out_ref[rows, cols] = (value[:, :HEAD] / value[:, HEAD:]).astype(BF16)


def attention(states, squares, bias, gain, sharp, width, start, rows):
    cols = states.shape[1]
    tile = min(rows, 256)
    first = start // tile
    sub = tile // GROUP
    return pl.pallas_call(
        functools.partial(attention_kernel, width),
        grid=(rows // tile,),
        in_specs=[
            pl.BlockSpec((tile, cols), lambda i: (first + i, 0)),
            pl.BlockSpec((1, sub, GROUP), lambda i: (first + i, 0, 0)),
            pl.BlockSpec((tile, GROUP), lambda i: (first + i, 0)),
            pl.BlockSpec((1, cols), lambda i: (0, 0)),
            pl.BlockSpec(memory_space=pltpu.SMEM),
        ],
        out_specs=pl.BlockSpec((tile, cols), lambda i: (i, 0)),
        out_shape=jax.ShapeDtypeStruct((rows, cols), BF16),
        compiler_params=params(16),
        cost_estimate=pl.CostEstimate(
            flops=rows * GROUP * cols * 16, bytes_accessed=rows * cols * 4, transcendentals=rows * GROUP * 4
        ),
        name="attention",
    )(states, squares.reshape(-1, sub, GROUP), bias, gain, sharp)


def product_kernel(pos_ref, *refs):
    mixed, (weight_ref, out_ref) = refs[:-2], refs[-2:]
    total = None
    for b, ref in enumerate(mixed):
        term = jnp.dot(ref[...], weight_ref[pos_ref[1 + b]], preferred_element_type=F32)
        total = term if total is None else total + term
    out_ref[...] = total.astype(out_ref.dtype)


def vmem():
    return pl.BlockSpec(memory_space=pltpu.VMEM)


def smem():
    return pl.BlockSpec(memory_space=pltpu.SMEM)


def product(pos, mixed, weight, dtype):
    blocks, depth, cols = weight.shape
    rows = mixed[0].shape[0]
    return pl.pallas_call(
        product_kernel,
        in_specs=[smem()] + [vmem()] * (len(mixed) + 1),
        out_specs=vmem(),
        out_shape=jax.ShapeDtypeStruct((rows, cols), dtype),
        compiler_params=params(24),
        cost_estimate=pl.CostEstimate(
            flops=2 * rows * blocks * depth * cols,
            bytes_accessed=2 * rows * blocks * depth + 2 * blocks * depth * cols,
            transcendentals=0,
        ),
        name="product",
    )(pos, *mixed, weight)


def gradient_kernel(chunks, has_acc, pos_ref, *refs):
    refs = list(refs)
    out_ref = refs.pop()
    acc_ref = refs.pop() if has_acc else None
    blocks = len(refs) // chunks - 2
    mixed = [refs[n * blocks : (n + 1) * blocks] for n in range(chunks)]
    grads = refs[chunks * blocks :]
    grads = [g[...].astype(F32).T.astype(BF16) for g in grads]
    halves = ((pos_ref[0], grads[:chunks]), (1 - pos_ref[0], grads[chunks:]))
    for b in range(blocks):
        place = pos_ref[1 + b]
        for half, grad in halves:
            value = acc_ref[place, half] if has_acc else None
            for n in range(chunks):
                term = jnp.dot(grad[n], mixed[n][b][...], preferred_element_type=F32)
                value = term if value is None else value + term
            out_ref[place, half] = value.astype(out_ref.dtype)


def gradient(pos, mixed, mine, other, acc, dtype):
    blocks = len(mixed[0])
    rows = sum(m[0].shape[0] for m in mixed)
    depth = mixed[0][0].shape[1]
    half = mine[0].shape[1]
    operands = [*(value for chunk in mixed for value in chunk), *mine, *other]
    if acc is not None:
        operands.append(acc)
    return pl.pallas_call(
        functools.partial(gradient_kernel, len(mixed), acc is not None),
        in_specs=[smem()] + [vmem()] * len(operands),
        out_specs=vmem(),
        out_shape=jax.ShapeDtypeStruct((blocks, 2, half, depth), dtype),
        compiler_params=params(40),
        cost_estimate=pl.CostEstimate(
            flops=4 * rows * blocks * depth * half,
            bytes_accessed=2 * rows * blocks * depth + 8 * blocks * depth * half,
            transcendentals=0,
        ),
        name="gradient",
    )(pos, *operands)


def after(value, *others):
    return lax.optimization_barrier((value, *others))[0]


def swap(value, axis):
    return lax.ppermute(value, axis, ring(2, 1))


def body(states, gain, sharpness, ancestor_ids, proposal, future):
    tokens, width = states.shape
    total_width = gain.shape[0]
    xh, xl = lax.axis_index("xh"), lax.axis_index("xl")
    y, c = lax.axis_index("y"), lax.axis_index("c")
    heads = width // HEAD

    order = [2 * ((y + dy) & 3) + (c ^ dc) for dc in (0, 1) for dy in (0, 3, 1, 2)]
    pos = jnp.stack([xl, *order]).astype(jnp.int32)
    place = 8 * xl + 2 * y + c
    my_gain = lax.dynamic_slice_in_dim(gain, place * width, width).reshape(1, width)
    my_sharp = lax.dynamic_slice_in_dim(sharpness, place * heads, heads).reshape(1, heads)
    bias = reach_bias(ancestor_ids.reshape(-1, GROUP))

    first = lax.ppermute(proposal, ("xh", "xl"), GATHER_A)
    second = lax.ppermute(proposal, ("xh", "xl"), GATHER_B)
    wide = states.astype(F32)
    squares = jnp.sum(wide * wide, axis=1).reshape(-1, GROUP)
    squares = squares + swap(squares, "c")
    squares = squares + swap(squares, "xl")
    first, second, squares = lax.optimization_barrier((first, second, squares))
    send_weight = lax.all_gather(jnp.where(xh == xl, first, second), "z", axis=0, tiled=False)
    keep_weight = lax.all_gather(jnp.where(xh == xl, proposal, first), "z", axis=0, tiled=False)
    squares = squares + sum(lax.ppermute(squares, "y", ring(4, k)) for k in (1, 2, 3))

    count = len(CHUNKS)
    starts = [sum(CHUNKS[:i]) for i in range(count)]
    mixed = [
        attention(states, squares, bias, my_gain, my_sharp, total_width, start, rows)
        for start, rows in zip(starts, CHUNKS)
    ]

    up, down, far = [], [], []
    for i in range(count):
        source = mixed[i]
        if i >= 2:
            source = after(source, up[i - 2], down[i - 2])
        up.append(lax.ppermute(source, "y", ring(4, 1)))
        down.append(lax.ppermute(source, "y", ring(4, -1)))

    def relay(i, *others):
        source, step = (up[i], 1) if FAR[i] else (down[i], -1)
        far.append(lax.ppermute(after(source, *others), "y", ring(4, step)))

    def blocks(i):
        here = (mixed[i], up[i], down[i], far[i])
        return [*here, *(swap(value, "c") for value in here)]

    def swapped(i):
        return swap(product(pos, full[i], send_weight, BF16), "xl")

    def receive(i, *others):
        kept = product(pos, [after(full[i][0], *others), *full[i][1:]], keep_weight, F32)
        result = kept + got[i].astype(F32)
        predicted.append(result.astype(BF16))
        target = lax.slice_in_dim(future, starts[i], starts[i] + CHUNKS[i]).astype(F32)
        mine.append(jnp.clip(result - target, -1.0, 1.0).astype(BF16))
        other.append(swap(mine[i], "xl"))

    predicted, full, got, mine, other = [], [], [], [], []
    relay(0)
    relay(1)
    full.append(blocks(0))
    full.append(blocks(1))
    relay(2)
    got.append(swapped(0))
    relay(3)
    got.append(swapped(1))
    full.append(blocks(2))
    got.append(swapped(2))
    receive(0, down[3], got[1])
    receive(1, got[2])
    full.append(blocks(3))
    full[3][0] = after(full[3][0], mine[1])
    got.append(swapped(3))
    receive(2, mine[1])
    receive(3, mine[2])
    full[0][0] = after(full[0][0], mine[3])
    acc = gradient(pos, full[:2], mine[:2], other[:2], None, F32)
    acc = gradient(pos, full[2:], mine[2:], other[2:], acc, BF16)

    summed = lax.psum_scatter(acc, "z", scatter_dimension=0, tiled=False)
    low, high = summed[0], summed[1]
    to_a = jnp.where(xh == 1, low, high)
    to_b = jnp.where(xh == 1, high, low)
    got_a = lax.ppermute(to_a, ("xh", "xl"), SCATTER_A)
    got_b = lax.ppermute(to_b, ("xh", "xl"), SCATTER_B)
    got_b = jnp.where(xh == xl, to_b, got_b)
    weight_grad = (got_a.astype(F32) + got_b.astype(F32)).T / math.sqrt(
        tokens * lax.axis_size("xh") * lax.axis_size("z")
    )
    return jnp.concatenate(predicted), weight_grad


def solution(mesh):
    grid = Mesh(mesh.devices.reshape(2, 8, 2, 4, 2), ("xh", "z", "xl", "y", "c"))
    dp, tensor = ("xh", "z"), ("xl", "y", "c")
    return jax.shard_map(
        body,
        mesh=grid,
        in_specs=(P(dp, tensor), P(), P(), P(dp), P(dp, tensor), P(dp, tensor)),
        out_specs=(P(dp, tensor), P(dp, tensor)),
        check_vma=False,
    )
```

```python
import functools
import math

import jax
import jax.numpy as jnp
from jax import lax
from jax.experimental import pallas as pl
from jax.experimental.pallas import tpu as pltpu
from jax.sharding import Mesh
from jax.sharding import PartitionSpec as P

HEAD = 128
BLOCK = 64
GROUP = 128
EPS = 1e-05
CHUNKS = (512, 512, 512, 512)
FAR = (True, False, True, False)
BF16 = jnp.bfloat16
F32 = jnp.float32

GATHER_A = ((0, 2), (1, 0), (2, 3), (3, 1))
GATHER_B = ((1, 2), (2, 1))
SCATTER_A = tuple((dst, src) for src, dst in GATHER_A)
SCATTER_B = GATHER_B


def ring(n, step):
    return [(i, (i + step) % n) for i in range(n)]


def params(mib=48):
    return pltpu.CompilerParams(vmem_limit_bytes=mib * 1024 * 1024)


def reach_kernel(ids_ref, bias_ref):
    groups = ids_ref.shape[0]
    row = lax.broadcasted_iota(jnp.int32, (GROUP, GROUP), 0)
    col = lax.broadcasted_iota(jnp.int32, (GROUP, GROUP), 1)
    base = jnp.where(col >= BLOCK, BLOCK, 0)
    inner = (col != 0) & (col != BLOCK)
    eye = row == col
    reach = []
    for g in range(groups):
        parent = ids_ref[g : g + 1, :] + base
        hit = ((parent == row) & inner) | eye
        reach.append(jnp.where(hit, 1.0, 0.0).astype(BF16))
    for sweep in range(6):
        reach = [
            jnp.minimum(jnp.dot(r, r, preferred_element_type=F32), 1.0).astype(BF16) for r in reach
        ]
    for g in range(groups):
        bias = jnp.where(reach[g].astype(F32) > 0.0, 0.0, -1e30)
        bias_ref[g * GROUP : (g + 1) * GROUP, :] = bias.T


def reach_bias(ids):
    groups = ids.shape[0]
    return pl.pallas_call(
        reach_kernel,
        out_shape=jax.ShapeDtypeStruct((groups * GROUP, GROUP), F32),
        compiler_params=params(16),
        cost_estimate=pl.CostEstimate(
            flops=groups * 6 * 2 * GROUP**3, bytes_accessed=groups * GROUP * GROUP * 4, transcendentals=0
        ),
        name="reach",
    )(ids)


def attention_kernel(width, x_ref, sq_ref, bias_ref, gain_ref, sharp_ref, out_ref):
    groups = x_ref.shape[0] // GROUP
    heads = x_ref.shape[1] // HEAD
    row = lax.broadcasted_iota(jnp.int32, (GROUP, GROUP), 0)
    col = lax.broadcasted_iota(jnp.int32, (GROUP, GROUP), 1)
    eye = row == col
    gain = gain_ref[...]
    ones = jnp.ones((GROUP, HEAD), BF16)
    where = [
        (slice(g * GROUP, (g + 1) * GROUP), slice(h * HEAD, (h + 1) * HEAD), h)
        for g in range(groups)
        for h in range(heads)
    ]
    feats = []
    for g in range(groups):
        rows = slice(g * GROUP, (g + 1) * GROUP)
        scale = lax.rsqrt(sq_ref[0, g : g + 1, :] * (1.0 / width) + EPS)
        scale = jnp.sum(jnp.where(eye, scale, 0.0), axis=1, keepdims=True)
        normed = (x_ref[rows, :].astype(F32) * scale * gain).astype(BF16)
        feats += [normed[:, h * HEAD : (h + 1) * HEAD] for h in range(heads)]
    factor = math.log2(math.e) / math.sqrt(HEAD)
    scores = [
        lax.dot_general(f, f, (((1,), (1,)), ((), ())), preferred_element_type=F32) for f in feats
    ]
    scores = [
        s * (sharp_ref[0, h] * factor) + bias_ref[rows, :] for s, (rows, _, h) in zip(scores, where)
    ]
    tops = [jnp.max(s, axis=1, keepdims=True) for s in scores]
    terms = [jnp.exp2(s - top).astype(BF16) for s, top in zip(scores, tops)]
    sums = [
        jnp.dot(t, jnp.concatenate([f, ones], axis=1), preferred_element_type=F32)
        for t, f in zip(terms, feats)
    ]
    for value, (rows, cols, _) in zip(sums, where):
        out_ref[rows, cols] = (value[:, :HEAD] / value[:, HEAD:]).astype(BF16)


def attention(states, squares, bias, gain, sharp, width, start, rows):
    cols = states.shape[1]
    tile = min(rows, 256)
    first = start // tile
    sub = tile // GROUP
    return pl.pallas_call(
        functools.partial(attention_kernel, width),
        grid=(rows // tile,),
        in_specs=[
            pl.BlockSpec((tile, cols), lambda i: (first + i, 0)),
            pl.BlockSpec((1, sub, GROUP), lambda i: (first + i, 0, 0)),
            pl.BlockSpec((tile, GROUP), lambda i: (first + i, 0)),
            pl.BlockSpec((1, cols), lambda i: (0, 0)),
            pl.BlockSpec(memory_space=pltpu.SMEM),
        ],
        out_specs=pl.BlockSpec((tile, cols), lambda i: (i, 0)),
        out_shape=jax.ShapeDtypeStruct((rows, cols), BF16),
        compiler_params=params(16),
        cost_estimate=pl.CostEstimate(
            flops=rows * GROUP * cols * 16, bytes_accessed=rows * cols * 4, transcendentals=rows * GROUP * 4
        ),
        name="attention",
    )(states, squares.reshape(-1, sub, GROUP), bias, gain, sharp)


def vmem():
    return pl.BlockSpec(memory_space=pltpu.VMEM)


def smem():
    return pl.BlockSpec(memory_space=pltpu.SMEM)


def hbm():
    return pl.BlockSpec(memory_space=pltpu.MemorySpace.HBM)


def forward_kernel(pos_ref, *refs):
    *mixed_refs, weight_ref, keep_ref, send_ref, mixed, weight, sems = refs
    loads = []
    for b, ref in enumerate(mixed_refs):
        pair = (
            pltpu.make_async_copy(ref, mixed.at[b], sems.at[0, b]),
            pltpu.make_async_copy(weight_ref.at[pos_ref[1 + b]], weight.at[b], sems.at[1, b]),
        )
        for load in pair:
            load.start()
        loads.append(pair)
    keep = send = None
    for b, pair in enumerate(loads):
        for load in pair:
            load.wait()
        value = mixed[b]
        kept = jnp.dot(value, weight[b, pos_ref[0]], preferred_element_type=F32)
        sent = jnp.dot(value, weight[b, 1 - pos_ref[0]], preferred_element_type=F32)
        keep = kept if b == 0 else keep + kept
        send = sent if b == 0 else send + sent
    keep_ref[...] = keep
    send_ref[...] = send.astype(BF16)


def forward(pos, mixed, weight):
    blocks, _, depth, cols = weight.shape
    rows = mixed[0].shape[0]
    return pl.pallas_call(
        forward_kernel,
        in_specs=[smem()] + [hbm()] * (len(mixed) + 1),
        out_specs=[vmem()] * 2,
        out_shape=[
            jax.ShapeDtypeStruct((rows, cols), F32),
            jax.ShapeDtypeStruct((rows, cols), BF16),
        ],
        scratch_shapes=[
            pltpu.VMEM((blocks, rows, depth), BF16),
            pltpu.VMEM(weight.shape, BF16),
            pltpu.SemaphoreType.DMA((2, blocks)),
        ],
        compiler_params=params(24),
        cost_estimate=pl.CostEstimate(
            flops=4 * rows * blocks * depth * cols,
            bytes_accessed=2 * rows * blocks * depth + 4 * blocks * depth * cols,
            transcendentals=0,
        ),
        name="forward",
    )(pos, *mixed, weight)


def gradient_kernel(chunks, blocks, has_acc, pos_ref, *refs):
    refs = list(refs)
    sources = [refs[n * blocks : (n + 1) * blocks] for n in range(chunks)]
    refs = refs[chunks * blocks :]
    grads, refs = refs[: 2 * chunks], refs[2 * chunks :]
    acc_ref = refs.pop(0) if has_acc else None
    out_ref, *mixed = refs[: 1 + chunks]
    refs = refs[1 + chunks :]
    acc = refs.pop(0) if has_acc else None
    out, sems = refs
    loads = []
    for b in range(blocks):
        step = [
            pltpu.make_async_copy(sources[n][b], mixed[n].at[b], sems.at[n, b])
            for n in range(chunks)
        ]
        if has_acc:
            step.append(
                pltpu.make_async_copy(acc_ref.at[pos_ref[1 + b]], acc.at[b], sems.at[chunks, b])
            )
        for load in step:
            load.start()
        loads.append(step)
    grads = [g[...].astype(F32).T.astype(BF16) for g in grads]
    halves = ((pos_ref[0], grads[:chunks]), (1 - pos_ref[0], grads[chunks:]))
    stores = []
    for b in range(blocks):
        for load in loads[b]:
            load.wait()
        for half, grad in halves:
            value = acc[b, half] if has_acc else None
            for n in range(chunks):
                term = jnp.dot(grad[n], mixed[n][b], preferred_element_type=F32)
                value = term if value is None else value + term
            out[b, half] = value.astype(out.dtype)
        store = pltpu.make_async_copy(out.at[b], out_ref.at[pos_ref[1 + b]], sems.at[chunks + 1, b])
        store.start()
        stores.append(store)
    for store in stores:
        store.wait()


def gradient(pos, mixed, mine, other, acc, dtype):
    chunks = len(mixed)
    blocks = len(mixed[0])
    rows = [m[0].shape[0] for m in mixed]
    depth = mixed[0][0].shape[1]
    half = mine[0].shape[1]
    shape = (blocks, 2, half, depth)
    operands = [*(value for chunk in mixed for value in chunk), *mine, *other]
    in_specs = [smem()] + [hbm()] * (chunks * blocks) + [vmem()] * (2 * chunks)
    scratch = [pltpu.VMEM((blocks, count, depth), BF16) for count in rows]
    if acc is not None:
        operands.append(acc)
        in_specs.append(hbm())
        scratch.append(pltpu.VMEM(shape, F32))
    scratch += [pltpu.VMEM(shape, dtype), pltpu.SemaphoreType.DMA((chunks + 2, blocks))]
    return pl.pallas_call(
        functools.partial(gradient_kernel, chunks, blocks, acc is not None),
        in_specs=in_specs,
        out_specs=hbm(),
        out_shape=jax.ShapeDtypeStruct(shape, dtype),
        scratch_shapes=scratch,
        compiler_params=params(40),
        cost_estimate=pl.CostEstimate(
            flops=4 * sum(rows) * blocks * depth * half,
            bytes_accessed=2 * sum(rows) * blocks * depth + 8 * blocks * depth * half,
            transcendentals=0,
        ),
        name="gradient",
    )(pos, *operands)


def after(value, *others):
    return lax.optimization_barrier((value, *others))[0]


def swap(value, axis):
    return lax.ppermute(value, axis, ring(2, 1))


def body(states, gain, sharpness, ancestor_ids, proposal, future):
    tokens, width = states.shape
    total_width = gain.shape[0]
    xh, xl = lax.axis_index("xh"), lax.axis_index("xl")
    y, c = lax.axis_index("y"), lax.axis_index("c")
    heads = width // HEAD

    order = [2 * ((y + dy) & 3) + (c ^ dc) for dc in (0, 1) for dy in (0, 3, 1, 2)]
    pos = jnp.stack([xl, *order]).astype(jnp.int32)
    place = 8 * xl + 2 * y + c
    my_gain = lax.dynamic_slice_in_dim(gain, place * width, width).reshape(1, width)
    my_sharp = lax.dynamic_slice_in_dim(sharpness, place * heads, heads).reshape(1, heads)
    bias = reach_bias(ancestor_ids.reshape(-1, GROUP))

    first = lax.ppermute(proposal, ("xh", "xl"), GATHER_A)
    second = lax.ppermute(proposal, ("xh", "xl"), GATHER_B)
    wide = states.astype(F32)
    squares = jnp.sum(wide * wide, axis=1).reshape(-1, GROUP)
    squares = squares + swap(squares, "c")
    there = swap(squares, "xl")
    there, bias, my_gain, my_sharp = lax.optimization_barrier((there, bias, my_gain, my_sharp))
    squares = squares + there
    first, second, squares = lax.optimization_barrier((first, second, squares))
    second = jnp.where(xh == xl, proposal, second)
    pair = jnp.stack([jnp.where(xh == 1, first, second), jnp.where(xh == 1, second, first)])
    weight = lax.all_gather(pair, "z", axis=0, tiled=False)
    squares = squares + sum(lax.ppermute(squares, "y", ring(4, k)) for k in (1, 2, 3))

    count = len(CHUNKS)
    starts = [sum(CHUNKS[:i]) for i in range(count)]
    mixed = [
        attention(states, squares, bias, my_gain, my_sharp, total_width, start, rows)
        for start, rows in zip(starts, CHUNKS)
    ]

    up, down, far = [], [], []
    for i in range(count):
        source = mixed[i]
        if i >= 2:
            source = after(source, up[i - 2], down[i - 2])
        up.append(lax.ppermute(source, "y", ring(4, 1)))
        down.append(lax.ppermute(source, "y", ring(4, -1)))

    def relay(i, *others):
        source, step = (up[i], 1) if FAR[i] else (down[i], -1)
        far.append(lax.ppermute(after(source, *others), "y", ring(4, step)))

    def blocks(i, *others):
        here = (mixed[i], up[i], down[i], far[i])
        swaps = [swap(value, "c") for value in here[:3]]
        return [*here, *swaps, swap(after(far[i], *others), "c")]

    def multiply(i):
        kept, sent = forward(pos, full[i], weight)
        keep.append(kept)
        send.append(sent)
        got.append(swap(sent, "xl"))

    def receive(i, *others):
        result = after(keep[i], *others) + got[i].astype(F32)
        predicted.append(result.astype(BF16))
        target = lax.slice_in_dim(future, starts[i], starts[i] + CHUNKS[i]).astype(F32)
        mine.append(jnp.clip(result - target, -1.0, 1.0).astype(BF16))
        other.append(swap(mine[i], "xl"))

    predicted, full, keep, send, got, mine, other = [], [], [], [], [], [], []
    relay(0)
    relay(1)
    full.append(blocks(0))
    full.append(blocks(1))
    relay(2)
    multiply(0)
    multiply(1)
    relay(3, send[0], send[1])
    receive(0)
    full.append(blocks(2))
    full[2][0] = after(full[2][0], mine[0])
    multiply(2)
    receive(1, send[2])
    full.append(blocks(3, mine[1]))
    multiply(3)
    receive(2, send[3])
    acc = gradient(pos, full[:2], mine[:2], [other[0], after(other[1], mine[2])], None, F32)
    receive(3)
    acc = gradient(pos, full[2:], mine[2:], other[2:], acc, BF16)

    summed = lax.psum_scatter(acc, "z", scatter_dimension=0, tiled=False)
    low, high = summed[0], summed[1]
    to_a = jnp.where(xh == 1, low, high)
    to_b = jnp.where(xh == 1, high, low)
    got_a = lax.ppermute(to_a, ("xh", "xl"), SCATTER_A)
    got_b = lax.ppermute(to_b, ("xh", "xl"), SCATTER_B)
    got_b = jnp.where(xh == xl, to_b, got_b)
    weight_grad = (got_a.astype(F32) + got_b.astype(F32)).T / math.sqrt(
        tokens * lax.axis_size("xh") * lax.axis_size("z")
    )
    return jnp.concatenate(predicted), weight_grad


def solution(mesh):
    grid = Mesh(mesh.devices.reshape(2, 8, 2, 4, 2), ("xh", "z", "xl", "y", "c"))
    dp, tensor = ("xh", "z"), ("xl", "y", "c")
    return jax.shard_map(
        body,
        mesh=grid,
        in_specs=(P(dp, tensor), P(), P(), P(dp), P(dp, tensor), P(dp, tensor)),
        out_specs=(P(dp, tensor), P(dp, tensor)),
        check_vma=False,
    )
```

```python
import functools
import math

import jax
import jax.numpy as jnp
from jax import lax
from jax.experimental import pallas as pl
from jax.experimental.pallas import tpu as pltpu
from jax.sharding import Mesh
from jax.sharding import PartitionSpec as P

HEAD = 128
BLOCK = 64
GROUP = 128
EPS = 1e-05
CHUNKS = (512, 512, 512, 512)
FAR = (True, False, True, False)
BF16 = jnp.bfloat16
F32 = jnp.float32

GATHER_A = ((0, 2), (1, 0), (2, 3), (3, 1))
GATHER_B = ((1, 2), (2, 1))
SCATTER_A = tuple((dst, src) for src, dst in GATHER_A)
SCATTER_B = GATHER_B


def ring(n, step):
    return [(i, (i + step) % n) for i in range(n)]


def params(mib=48):
    return pltpu.CompilerParams(vmem_limit_bytes=mib * 1024 * 1024)


def reach_kernel(ids_ref, bias_ref):
    groups = ids_ref.shape[0]
    row = lax.broadcasted_iota(jnp.int32, (GROUP, GROUP), 0)
    col = lax.broadcasted_iota(jnp.int32, (GROUP, GROUP), 1)
    base = jnp.where(col >= BLOCK, BLOCK, 0)
    inner = (col != 0) & (col != BLOCK)
    eye = row == col
    reach = []
    for g in range(groups):
        parent = ids_ref[g : g + 1, :] + base
        hit = ((parent == row) & inner) | eye
        reach.append(jnp.where(hit, 1.0, 0.0).astype(BF16))
    for sweep in range(6):
        reach = [
            jnp.minimum(jnp.dot(r, r, preferred_element_type=F32), 1.0).astype(BF16) for r in reach
        ]
    for g in range(groups):
        bias = jnp.where(reach[g].astype(F32) > 0.0, 0.0, -1e30)
        bias_ref[g * GROUP : (g + 1) * GROUP, :] = bias.T


def reach_bias(ids):
    groups = ids.shape[0]
    return pl.pallas_call(
        reach_kernel,
        out_shape=jax.ShapeDtypeStruct((groups * GROUP, GROUP), F32),
        compiler_params=params(16),
        cost_estimate=pl.CostEstimate(
            flops=groups * 6 * 2 * GROUP**3, bytes_accessed=groups * GROUP * GROUP * 4, transcendentals=0
        ),
        name="reach",
    )(ids)


def attention_kernel(width, x_ref, sq_ref, bias_ref, gain_ref, sharp_ref, out_ref):
    groups = x_ref.shape[0] // GROUP
    heads = x_ref.shape[1] // HEAD
    row = lax.broadcasted_iota(jnp.int32, (GROUP, GROUP), 0)
    col = lax.broadcasted_iota(jnp.int32, (GROUP, GROUP), 1)
    eye = row == col
    gain = gain_ref[...]
    ones = jnp.ones((GROUP, HEAD), BF16)
    where = [
        (slice(g * GROUP, (g + 1) * GROUP), slice(h * HEAD, (h + 1) * HEAD), h)
        for g in range(groups)
        for h in range(heads)
    ]
    feats = []
    for g in range(groups):
        rows = slice(g * GROUP, (g + 1) * GROUP)
        scale = lax.rsqrt(sq_ref[0, g : g + 1, :] * (1.0 / width) + EPS)
        scale = jnp.sum(jnp.where(eye, scale, 0.0), axis=1, keepdims=True)
        normed = (x_ref[rows, :].astype(F32) * scale * gain).astype(BF16)
        feats += [normed[:, h * HEAD : (h + 1) * HEAD] for h in range(heads)]
    factor = math.log2(math.e) / math.sqrt(HEAD)
    scores = [
        lax.dot_general(f, f, (((1,), (1,)), ((), ())), preferred_element_type=F32) for f in feats
    ]
    scores = [
        s * (sharp_ref[0, h] * factor) + bias_ref[rows, :] for s, (rows, _, h) in zip(scores, where)
    ]
    tops = [jnp.max(s, axis=1, keepdims=True) for s in scores]
    terms = [jnp.exp2(s - top).astype(BF16) for s, top in zip(scores, tops)]
    sums = [
        jnp.dot(t, jnp.concatenate([f, ones], axis=1), preferred_element_type=F32)
        for t, f in zip(terms, feats)
    ]
    for value, (rows, cols, _) in zip(sums, where):
        out_ref[rows, cols] = (value[:, :HEAD] / value[:, HEAD:]).astype(BF16)


def attention(states, squares, bias, gain, sharp, width, start, rows):
    cols = states.shape[1]
    tile = min(rows, 256)
    first = start // tile
    sub = tile // GROUP
    return pl.pallas_call(
        functools.partial(attention_kernel, width),
        grid=(rows // tile,),
        in_specs=[
            pl.BlockSpec((tile, cols), lambda i: (first + i, 0)),
            pl.BlockSpec((1, sub, GROUP), lambda i: (first + i, 0, 0)),
            pl.BlockSpec((tile, GROUP), lambda i: (first + i, 0)),
            pl.BlockSpec((1, cols), lambda i: (0, 0)),
            pl.BlockSpec(memory_space=pltpu.SMEM),
        ],
        out_specs=pl.BlockSpec((tile, cols), lambda i: (i, 0)),
        out_shape=jax.ShapeDtypeStruct((rows, cols), BF16),
        compiler_params=params(16),
        cost_estimate=pl.CostEstimate(
            flops=rows * GROUP * cols * 16, bytes_accessed=rows * cols * 4, transcendentals=rows * GROUP * 4
        ),
        name="attention",
    )(states, squares.reshape(-1, sub, GROUP), bias, gain, sharp)


def vmem():
    return pl.BlockSpec(memory_space=pltpu.VMEM)


def smem():
    return pl.BlockSpec(memory_space=pltpu.SMEM)


def hbm():
    return pl.BlockSpec(memory_space=pltpu.MemorySpace.HBM)


def forward_kernel(pos_ref, *refs):
    *mixed_refs, weight_ref, keep_ref, send_ref, mixed, weight, sems = refs
    loads = []
    for b, ref in enumerate(mixed_refs):
        pair = (
            pltpu.make_async_copy(ref, mixed.at[b], sems.at[0, b]),
            pltpu.make_async_copy(weight_ref.at[pos_ref[1 + b]], weight.at[b], sems.at[1, b]),
        )
        for load in pair:
            load.start()
        loads.append(pair)
    total = None
    for b, pair in enumerate(loads):
        for load in pair:
            load.wait()
        term = jnp.dot(mixed[b], weight[b], preferred_element_type=F32)
        total = term if total is None else total + term
    half = keep_ref.shape[1]
    send_ref[...] = total[:, half:].astype(BF16)
    keep_ref[...] = total[:, :half]


def forward(pos, mixed, weight):
    blocks, depth, cols = weight.shape
    cols = cols // 2
    rows = mixed[0].shape[0]
    return pl.pallas_call(
        forward_kernel,
        in_specs=[smem()] + [hbm()] * (len(mixed) + 1),
        out_specs=[vmem()] * 2,
        out_shape=[
            jax.ShapeDtypeStruct((rows, cols), F32),
            jax.ShapeDtypeStruct((rows, cols), BF16),
        ],
        scratch_shapes=[
            pltpu.VMEM((blocks, rows, depth), BF16),
            pltpu.VMEM(weight.shape, BF16),
            pltpu.SemaphoreType.DMA((2, blocks)),
        ],
        compiler_params=params(60),
        cost_estimate=pl.CostEstimate(
            flops=4 * rows * blocks * depth * cols,
            bytes_accessed=2 * rows * blocks * depth + 4 * blocks * depth * cols,
            transcendentals=0,
        ),
        name="forward",
    )(pos, *mixed, weight)


def gradient_kernel(chunks, blocks, has_acc, pos_ref, *refs):
    refs = list(refs)
    sources = [refs[n * blocks : (n + 1) * blocks] for n in range(chunks)]
    refs = refs[chunks * blocks :]
    grads, refs = refs[: 2 * chunks], refs[2 * chunks :]
    acc_ref = refs.pop(0) if has_acc else None
    out_ref, *mixed = refs[: 1 + chunks]
    refs = refs[1 + chunks :]
    acc = refs.pop(0) if has_acc else None
    out, sems = refs
    size = out.shape[1]

    def place(ref, b):
        return ref.at[pl.ds(pl.multiple_of(pos_ref[1 + b] * size, size), size)]

    loads = []
    for b in range(blocks):
        step = [
            pltpu.make_async_copy(sources[n][b], mixed[n].at[b], sems.at[n, b])
            for n in range(chunks)
        ]
        if has_acc:
            step.append(
                pltpu.make_async_copy(place(acc_ref, b), acc.at[b], sems.at[chunks, b])
            )
        for load in step:
            load.start()
        loads.append(step)
    grads = [g[...].astype(F32).T.astype(BF16) for g in grads]
    first = pos_ref[0] * (size // 2)
    halves = ((first, grads[:chunks]), (size // 2 - first, grads[chunks:]))
    stores = []
    for b in range(blocks):
        for load in loads[b]:
            load.wait()
        for start, grad in halves:
            rows = pl.ds(pl.multiple_of(start, size // 2), size // 2)
            value = acc[b, rows, :] if has_acc else None
            for n in range(chunks):
                term = jnp.dot(grad[n], mixed[n][b], preferred_element_type=F32)
                value = term if value is None else value + term
            out[b, rows, :] = value.astype(out.dtype)
        store = pltpu.make_async_copy(out.at[b], place(out_ref, b), sems.at[chunks + 1, b])
        store.start()
        stores.append(store)
    for store in stores:
        store.wait()


def gradient(pos, mixed, mine, other, acc, dtype):
    chunks = len(mixed)
    blocks = len(mixed[0])
    rows = [m[0].shape[0] for m in mixed]
    depth = mixed[0][0].shape[1]
    half = mine[0].shape[1]
    shape = (blocks, 2 * half, depth)
    operands = [*(value for chunk in mixed for value in chunk), *mine, *other]
    in_specs = [smem()] + [hbm()] * (chunks * blocks) + [vmem()] * (2 * chunks)
    scratch = [pltpu.VMEM((blocks, count, depth), BF16) for count in rows]
    if acc is not None:
        operands.append(acc)
        in_specs.append(hbm())
        scratch.append(pltpu.VMEM(shape, F32))
    scratch += [pltpu.VMEM(shape, dtype), pltpu.SemaphoreType.DMA((chunks + 2, blocks))]
    return pl.pallas_call(
        functools.partial(gradient_kernel, chunks, blocks, acc is not None),
        in_specs=in_specs,
        out_specs=hbm(),
        out_shape=jax.ShapeDtypeStruct((blocks * 2 * half, depth), dtype),
        scratch_shapes=scratch,
        compiler_params=params(60),
        cost_estimate=pl.CostEstimate(
            flops=4 * sum(rows) * blocks * depth * half,
            bytes_accessed=2 * sum(rows) * blocks * depth + 8 * blocks * depth * half,
            transcendentals=0,
        ),
        name="gradient",
    )(pos, *operands)


def after(value, *others):
    return lax.optimization_barrier((value, *others))[0]


def swap(value, axis):
    return lax.ppermute(value, axis, ring(2, 1))


def body(states, gain, sharpness, ancestor_ids, proposal, future):
    tokens, width = states.shape
    total_width = gain.shape[0]
    xh, xl = lax.axis_index("xh"), lax.axis_index("xl")
    y, c = lax.axis_index("y"), lax.axis_index("c")
    heads = width // HEAD

    order = [2 * ((y + dy) & 3) + (c ^ dc) for dc in (0, 1) for dy in (0, 3, 1, 2)]
    pos = jnp.stack([1 - (xl ^ xh), *order]).astype(jnp.int32)
    place = 8 * xl + 2 * y + c
    my_gain = lax.dynamic_slice_in_dim(gain, place * width, width).reshape(1, width)
    my_sharp = lax.dynamic_slice_in_dim(sharpness, place * heads, heads).reshape(1, heads)
    bias = reach_bias(ancestor_ids.reshape(-1, GROUP))

    first = lax.ppermute(proposal, ("xh", "xl"), GATHER_A)
    second = lax.ppermute(proposal, ("xh", "xl"), GATHER_B)
    wide = states.astype(F32)
    squares = jnp.sum(wide * wide, axis=1).reshape(-1, GROUP)
    squares = squares + swap(squares, "c")
    there = swap(squares, "xl")
    there, bias, my_gain, my_sharp = lax.optimization_barrier((there, bias, my_gain, my_sharp))
    squares = squares + there
    first, second, squares = lax.optimization_barrier((first, second, squares))
    kept = jnp.where(xh == xl, proposal, first)
    sent = jnp.where(xh == xl, first, second)
    weight = lax.all_gather(jnp.concatenate([kept, sent], axis=1), "z", axis=0, tiled=False)
    squares = squares + sum(lax.ppermute(squares, "y", ring(4, k)) for k in (1, 2, 3))

    count = len(CHUNKS)
    starts = [sum(CHUNKS[:i]) for i in range(count)]
    mixed, up, down, far = [], [], [], []
    for i, (start, rows) in enumerate(zip(starts, CHUNKS)):
        if i >= 1:
            squares = after(squares, mixed[0], *up[: min(i - 1, 1)])
        source = attention(states, squares, bias, my_gain, my_sharp, total_width, start, rows)
        if i >= 2:
            source = after(source, up[i - 2], down[i - 2])
        mixed.append(source)
        up.append(lax.ppermute(source, "y", ring(4, 1)))
        down.append(lax.ppermute(source, "y", ring(4, -1)))

    def relay(i, *others):
        source, step = (up[i], 1) if FAR[i] else (down[i], -1)
        far.append(lax.ppermute(after(source, *others), "y", ring(4, step)))

    def blocks(i, *others):
        here = (mixed[i], up[i], down[i], far[i])
        swaps = [swap(value, "c") for value in here[:3]]
        return [*here, *swaps, swap(after(far[i], *others), "c")]

    def multiply(i):
        kept, sent = forward(pos, full[i], weight)
        keep.append(kept)
        send.append(sent)
        got.append(swap(sent, "xl"))

    def receive(i, *others):
        result = after(keep[i], *others) + got[i].astype(F32)
        predicted.append(result.astype(BF16))
        target = lax.slice_in_dim(future, starts[i], starts[i] + CHUNKS[i]).astype(F32)
        mine.append(jnp.clip(result - target, -1.0, 1.0).astype(BF16))
        other.append(swap(mine[i], "xl"))

    predicted, full, keep, send, got, mine, other = [], [], [], [], [], [], []
    relay(0)
    relay(1)
    full.append(blocks(0))
    full.append(blocks(1))
    relay(2)
    relay(3)
    full[0][0] = after(full[0][0], up[3], down[3])
    multiply(0)
    multiply(1)
    receive(0)
    full.append(blocks(2))
    full[2][0] = after(full[2][0], mine[0])
    multiply(2)
    receive(1, send[2])
    full.append(blocks(3, mine[1]))
    multiply(3)
    receive(2, send[3])
    receive(3)
    other[0] = after(other[0], mine[3])
    acc = gradient(pos, full[:2], mine[:2], other[:2], None, F32)
    acc = gradient(pos, full[2:], mine[2:], other[2:], acc, BF16)

    summed = lax.psum_scatter(acc, "z", scatter_dimension=0, tiled=True)
    to_a, to_b = jnp.split(summed, 2)
    got_a = lax.ppermute(to_a, ("xh", "xl"), SCATTER_A)
    got_b = lax.ppermute(to_b, ("xh", "xl"), SCATTER_B)
    got_b = jnp.where(xh == xl, to_b, got_b)
    weight_grad = (got_a.astype(F32) + got_b.astype(F32)).T / math.sqrt(
        tokens * lax.axis_size("xh") * lax.axis_size("z")
    )
    return jnp.concatenate(predicted), weight_grad


def solution(mesh):
    grid = Mesh(mesh.devices.reshape(2, 8, 2, 4, 2), ("xh", "z", "xl", "y", "c"))
    dp, tensor = ("xh", "z"), ("xl", "y", "c")
    return jax.shard_map(
        body,
        mesh=grid,
        in_specs=(P(dp, tensor), P(), P(), P(dp), P(dp, tensor), P(dp, tensor)),
        out_specs=(P(dp, tensor), P(dp, tensor)),
        check_vma=False,
    )
```

```python
import functools
import math

import jax
import jax.numpy as jnp
from jax import lax
from jax.experimental import pallas as pl
from jax.experimental.pallas import tpu as pltpu
from jax.sharding import Mesh
from jax.sharding import PartitionSpec as P

HEAD = 128
BLOCK = 64
GROUP = 128
EPS = 1e-05
CHUNKS = (512, 512, 512, 512)
FAR = (True, False, True, False)
BF16 = jnp.bfloat16
F32 = jnp.float32

GATHER_A = ((0, 2), (1, 0), (2, 3), (3, 1))
GATHER_B = ((1, 2), (2, 1))
SCATTER_A = tuple((dst, src) for src, dst in GATHER_A)
SCATTER_B = GATHER_B


def ring(n, step):
    return [(i, (i + step) % n) for i in range(n)]


def params(mib=48):
    return pltpu.CompilerParams(vmem_limit_bytes=mib * 1024 * 1024)


def reach_kernel(ids_ref, bias_ref):
    groups = ids_ref.shape[0]
    row = lax.broadcasted_iota(jnp.int32, (GROUP, GROUP), 0)
    col = lax.broadcasted_iota(jnp.int32, (GROUP, GROUP), 1)
    base = jnp.where(col >= BLOCK, BLOCK, 0)
    inner = (col != 0) & (col != BLOCK)
    eye = row == col
    reach = []
    for g in range(groups):
        parent = ids_ref[g : g + 1, :] + base
        hit = ((parent == row) & inner) | eye
        reach.append(jnp.where(hit, 1.0, 0.0).astype(BF16))
    for sweep in range(6):
        reach = [
            jnp.minimum(jnp.dot(r, r, preferred_element_type=F32), 1.0).astype(BF16) for r in reach
        ]
    for g in range(groups):
        bias = jnp.where(reach[g].astype(F32) > 0.0, 0.0, -1e30)
        bias_ref[g * GROUP : (g + 1) * GROUP, :] = bias.T


def reach_bias(ids):
    groups = ids.shape[0]
    return pl.pallas_call(
        reach_kernel,
        out_shape=jax.ShapeDtypeStruct((groups * GROUP, GROUP), F32),
        compiler_params=params(16),
        cost_estimate=pl.CostEstimate(
            flops=groups * 6 * 2 * GROUP**3, bytes_accessed=groups * GROUP * GROUP * 4, transcendentals=0
        ),
        name="reach",
    )(ids)


def attention_kernel(width, x_ref, sq_ref, bias_ref, gain_ref, sharp_ref, out_ref):
    groups = x_ref.shape[0] // GROUP
    heads = x_ref.shape[1] // HEAD
    row = lax.broadcasted_iota(jnp.int32, (GROUP, GROUP), 0)
    col = lax.broadcasted_iota(jnp.int32, (GROUP, GROUP), 1)
    eye = row == col
    gain = gain_ref[...]
    ones = jnp.ones((GROUP, HEAD), BF16)
    where = [
        (slice(g * GROUP, (g + 1) * GROUP), slice(h * HEAD, (h + 1) * HEAD), h)
        for g in range(groups)
        for h in range(heads)
    ]
    feats = []
    for g in range(groups):
        rows = slice(g * GROUP, (g + 1) * GROUP)
        scale = lax.rsqrt(sq_ref[0, g : g + 1, :] * (1.0 / width) + EPS)
        scale = jnp.sum(jnp.where(eye, scale, 0.0), axis=1, keepdims=True)
        normed = (x_ref[rows, :].astype(F32) * scale * gain).astype(BF16)
        feats += [normed[:, h * HEAD : (h + 1) * HEAD] for h in range(heads)]
    factor = math.log2(math.e) / math.sqrt(HEAD)
    scores = [
        lax.dot_general(f, f, (((1,), (1,)), ((), ())), preferred_element_type=F32) for f in feats
    ]
    scores = [
        s * (sharp_ref[0, h] * factor) + bias_ref[rows, :] for s, (rows, _, h) in zip(scores, where)
    ]
    tops = [jnp.max(s, axis=1, keepdims=True) for s in scores]
    terms = [jnp.exp2(s - top).astype(BF16) for s, top in zip(scores, tops)]
    sums = [
        jnp.dot(t, jnp.concatenate([f, ones], axis=1), preferred_element_type=F32)
        for t, f in zip(terms, feats)
    ]
    for value, (rows, cols, _) in zip(sums, where):
        out_ref[rows, cols] = (value[:, :HEAD] / value[:, HEAD:]).astype(BF16)


def attention(states, squares, bias, gain, sharp, width, start, rows):
    cols = states.shape[1]
    tile = min(rows, 256)
    first = start // tile
    sub = tile // GROUP
    return pl.pallas_call(
        functools.partial(attention_kernel, width),
        grid=(rows // tile,),
        in_specs=[
            pl.BlockSpec((tile, cols), lambda i: (first + i, 0)),
            pl.BlockSpec((1, sub, GROUP), lambda i: (first + i, 0, 0)),
            pl.BlockSpec((tile, GROUP), lambda i: (first + i, 0)),
            pl.BlockSpec((1, cols), lambda i: (0, 0)),
            pl.BlockSpec(memory_space=pltpu.SMEM),
        ],
        out_specs=pl.BlockSpec((tile, cols), lambda i: (i, 0)),
        out_shape=jax.ShapeDtypeStruct((rows, cols), BF16),
        compiler_params=params(16),
        cost_estimate=pl.CostEstimate(
            flops=rows * GROUP * cols * 16, bytes_accessed=rows * cols * 4, transcendentals=rows * GROUP * 4
        ),
        name="attention",
    )(states, squares.reshape(-1, sub, GROUP), bias, gain, sharp)


def vmem():
    return pl.BlockSpec(memory_space=pltpu.VMEM)


def smem():
    return pl.BlockSpec(memory_space=pltpu.SMEM)


def hbm():
    return pl.BlockSpec(memory_space=pltpu.MemorySpace.HBM)


def forward_kernel(pos_ref, *refs):
    *mixed_refs, weight_ref, keep_ref, send_ref, mixed, weight, sems = refs
    loads = []
    for b, ref in enumerate(mixed_refs):
        pair = (
            pltpu.make_async_copy(ref, mixed.at[b], sems.at[0, b]),
            pltpu.make_async_copy(weight_ref.at[pos_ref[1 + b]], weight.at[b], sems.at[1, b]),
        )
        for load in pair:
            load.start()
        loads.append(pair)
    total = None
    for b, pair in enumerate(loads):
        for load in pair:
            load.wait()
        term = jnp.dot(mixed[b], weight[b], preferred_element_type=F32)
        total = term if total is None else total + term
    half = keep_ref.shape[1]
    send_ref[...] = total[:, half:].astype(BF16)
    keep_ref[...] = total[:, :half]


def forward(pos, mixed, weight):
    blocks, depth, cols = weight.shape
    cols = cols // 2
    rows = mixed[0].shape[0]
    return pl.pallas_call(
        forward_kernel,
        in_specs=[smem()] + [hbm()] * (len(mixed) + 1),
        out_specs=[vmem()] * 2,
        out_shape=[
            jax.ShapeDtypeStruct((rows, cols), F32),
            jax.ShapeDtypeStruct((rows, cols), BF16),
        ],
        scratch_shapes=[
            pltpu.VMEM((blocks, rows, depth), BF16),
            pltpu.VMEM(weight.shape, BF16),
            pltpu.SemaphoreType.DMA((2, blocks)),
        ],
        compiler_params=params(60),
        cost_estimate=pl.CostEstimate(
            flops=4 * rows * blocks * depth * cols,
            bytes_accessed=2 * rows * blocks * depth + 4 * blocks * depth * cols,
            transcendentals=0,
        ),
        name="forward",
    )(pos, *mixed, weight)


def residual_kernel(keep_ref, got_ref, target_ref, predicted_ref, grad_ref):
    result = keep_ref[...] + got_ref[...].astype(F32)
    predicted_ref[...] = result.astype(BF16)
    grad_ref[...] = jnp.clip(result - target_ref[...].astype(F32), -1.0, 1.0).astype(BF16)


def residual(keep, got, future, start):
    rows, cols = keep.shape
    tile = min(rows, 256)
    here = pl.BlockSpec((tile, cols), lambda i: (i, 0))
    return pl.pallas_call(
        residual_kernel,
        grid=(rows // tile,),
        in_specs=[here, here, pl.BlockSpec((tile, cols), lambda i: (start // tile + i, 0))],
        out_specs=[here, here],
        out_shape=[jax.ShapeDtypeStruct((rows, cols), BF16)] * 2,
        compiler_params=params(8),
        cost_estimate=pl.CostEstimate(
            flops=4 * rows * cols, bytes_accessed=12 * rows * cols, transcendentals=0
        ),
        name="residual",
    )(keep, got, future)


def gradient_kernel(chunks, blocks, has_acc, pos_ref, *refs):
    refs = list(refs)
    sources = [refs[n * blocks : (n + 1) * blocks] for n in range(chunks)]
    refs = refs[chunks * blocks :]
    grads, refs = refs[: 2 * chunks], refs[2 * chunks :]
    acc_ref = refs.pop(0) if has_acc else None
    out_ref, *mixed = refs[: 1 + chunks]
    refs = refs[1 + chunks :]
    acc = refs.pop(0) if has_acc else None
    out, sems = refs
    size = out.shape[1]

    def place(ref, b):
        return ref.at[pl.ds(pl.multiple_of(pos_ref[1 + b] * size, size), size)]

    loads = []
    for b in range(blocks):
        step = [
            pltpu.make_async_copy(sources[n][b], mixed[n].at[b], sems.at[n, b])
            for n in range(chunks)
        ]
        if has_acc:
            step.append(
                pltpu.make_async_copy(place(acc_ref, b), acc.at[b], sems.at[chunks, b])
            )
        for load in step:
            load.start()
        loads.append(step)
    grads = [g[...].astype(F32).T.astype(BF16) for g in grads]
    first = pos_ref[0] * (size // 2)
    halves = ((first, grads[:chunks]), (size // 2 - first, grads[chunks:]))
    stores = []
    for b in range(blocks):
        for load in loads[b]:
            load.wait()
        for start, grad in halves:
            rows = pl.ds(pl.multiple_of(start, size // 2), size // 2)
            value = acc[b, rows, :] if has_acc else None
            for n in range(chunks):
                term = jnp.dot(grad[n], mixed[n][b], preferred_element_type=F32)
                value = term if value is None else value + term
            out[b, rows, :] = value.astype(out.dtype)
        store = pltpu.make_async_copy(out.at[b], place(out_ref, b), sems.at[chunks + 1, b])
        store.start()
        stores.append(store)
    for store in stores:
        store.wait()


def gradient(pos, mixed, mine, other, acc, dtype):
    chunks = len(mixed)
    blocks = len(mixed[0])
    rows = [m[0].shape[0] for m in mixed]
    depth = mixed[0][0].shape[1]
    half = mine[0].shape[1]
    shape = (blocks, 2 * half, depth)
    operands = [*(value for chunk in mixed for value in chunk), *mine, *other]
    in_specs = [smem()] + [hbm()] * (chunks * blocks) + [vmem()] * (2 * chunks)
    scratch = [pltpu.VMEM((blocks, count, depth), BF16) for count in rows]
    if acc is not None:
        operands.append(acc)
        in_specs.append(hbm())
        scratch.append(pltpu.VMEM(shape, F32))
    scratch += [pltpu.VMEM(shape, dtype), pltpu.SemaphoreType.DMA((chunks + 2, blocks))]
    return pl.pallas_call(
        functools.partial(gradient_kernel, chunks, blocks, acc is not None),
        in_specs=in_specs,
        out_specs=hbm(),
        out_shape=jax.ShapeDtypeStruct((blocks * 2 * half, depth), dtype),
        scratch_shapes=scratch,
        compiler_params=params(60),
        cost_estimate=pl.CostEstimate(
            flops=4 * sum(rows) * blocks * depth * half,
            bytes_accessed=2 * sum(rows) * blocks * depth + 8 * blocks * depth * half,
            transcendentals=0,
        ),
        name="gradient",
    )(pos, *operands)


def after(value, *others):
    return lax.optimization_barrier((value, *others))[0]


def swap(value, axis):
    return lax.ppermute(value, axis, ring(2, 1))


def body(states, gain, sharpness, ancestor_ids, proposal, future):
    tokens, width = states.shape
    total_width = gain.shape[0]
    xh, xl = lax.axis_index("xh"), lax.axis_index("xl")
    y, c = lax.axis_index("y"), lax.axis_index("c")
    heads = width // HEAD

    order = [2 * ((y + dy) & 3) + (c ^ dc) for dc in (0, 1) for dy in (0, 3, 1, 2)]
    pos = jnp.stack([1 - (xl ^ xh), *order]).astype(jnp.int32)
    place = 8 * xl + 2 * y + c
    my_gain = lax.dynamic_slice_in_dim(gain, place * width, width).reshape(1, width)
    my_sharp = lax.dynamic_slice_in_dim(sharpness, place * heads, heads).reshape(1, heads)
    bias = reach_bias(ancestor_ids.reshape(-1, GROUP))

    first = lax.ppermute(proposal, ("xh", "xl"), GATHER_A)
    second = lax.ppermute(proposal, ("xh", "xl"), GATHER_B)
    wide = states.astype(F32)
    squares = jnp.sum(wide * wide, axis=1).reshape(-1, GROUP)
    squares = squares + swap(squares, "c")
    there = swap(squares, "xl")
    there, bias, my_gain, my_sharp = lax.optimization_barrier((there, bias, my_gain, my_sharp))
    squares = squares + there
    first, second, squares = lax.optimization_barrier((first, second, squares))
    kept = jnp.where(xh == xl, proposal, first)
    sent = jnp.where(xh == xl, first, second)
    weight = lax.all_gather(jnp.concatenate([kept, sent], axis=1), "z", axis=0, tiled=False)
    squares = squares + sum(lax.ppermute(squares, "y", ring(4, k)) for k in (1, 2, 3))

    count = len(CHUNKS)
    starts = [sum(CHUNKS[:i]) for i in range(count)]
    mixed, up, down, far = [], [], [], []
    for i, (start, rows) in enumerate(zip(starts, CHUNKS)):
        if i >= 1:
            squares = after(squares, mixed[0], *up[: min(i - 1, 1)])
        source = attention(states, squares, bias, my_gain, my_sharp, total_width, start, rows)
        if i >= 2:
            source = after(source, up[i - 2], down[i - 2])
        mixed.append(source)
        up.append(lax.ppermute(source, "y", ring(4, 1)))
        down.append(lax.ppermute(source, "y", ring(4, -1)))

    def relay(i, *others):
        source, step = (up[i], 1) if FAR[i] else (down[i], -1)
        far.append(lax.ppermute(after(source, *others), "y", ring(4, step)))

    def blocks(i, *others):
        here = (mixed[i], up[i], down[i], far[i])
        return [*here, *(swap(after(value, *others), "c") for value in here)]

    def multiply(i):
        kept, sent = forward(pos, full[i], weight)
        keep.append(kept)
        send.append(sent)
        got.append(swap(sent, "xl"))

    def receive(i, *others):
        value, grad = residual(after(keep[i], *others), got[i], future, starts[i])
        predicted.append(value)
        mine.append(grad)
        other.append(swap(mine[i], "xl"))

    predicted, full, keep, send, got, mine, other = [], [], [], [], [], [], []
    relay(0)
    relay(1)
    full.append(blocks(0))
    full.append(blocks(1))
    relay(2)
    relay(3)
    full[0][0] = after(full[0][0], up[2], down[2])
    multiply(0)
    full[1][0] = after(full[1][0], send[0], up[3], down[3])
    multiply(1)
    full.append(blocks(2, send[1]))
    receive(0, send[1])
    receive(1)
    full[2][0] = after(full[2][0], other[0], mine[1])
    multiply(2)
    full.append(blocks(3, send[1], mine[0]))
    full[3][0] = after(full[3][0], send[2])
    multiply(3)
    receive(2, send[3])
    acc = gradient(pos, full[:2], mine[:2], [other[0], after(other[1], mine[2])], None, F32)
    receive(3, acc)
    acc = gradient(pos, full[2:], mine[2:], other[2:], acc, BF16)

    summed = lax.psum_scatter(acc, "z", scatter_dimension=0, tiled=True)
    to_a, to_b = jnp.split(summed, 2)
    got_a = lax.ppermute(to_a, ("xh", "xl"), SCATTER_A)
    got_b = lax.ppermute(to_b, ("xh", "xl"), SCATTER_B)
    got_b = jnp.where(xh == xl, to_b, got_b)
    weight_grad = (got_a.astype(F32) + got_b.astype(F32)).T / math.sqrt(
        tokens * lax.axis_size("xh") * lax.axis_size("z")
    )
    return jnp.concatenate(predicted), weight_grad


def solution(mesh):
    grid = Mesh(mesh.devices.reshape(2, 8, 2, 4, 2), ("xh", "z", "xl", "y", "c"))
    dp, tensor = ("xh", "z"), ("xl", "y", "c")
    return jax.shard_map(
        body,
        mesh=grid,
        in_specs=(P(dp, tensor), P(), P(), P(dp), P(dp, tensor), P(dp, tensor)),
        out_specs=(P(dp, tensor), P(dp, tensor)),
        check_vma=False,
    )
```

```python
import functools
import math

import jax
import jax.numpy as jnp
from jax import lax
from jax.experimental import pallas as pl
from jax.experimental.pallas import tpu as pltpu
from jax.sharding import Mesh
from jax.sharding import PartitionSpec as P

HEAD = 128
BLOCK = 64
GROUP = 128
EPS = 1e-05
CHUNKS = (512, 512, 512, 512)
FAR = (True, False, True, False)
BF16 = jnp.bfloat16
F32 = jnp.float32

GATHER_A = ((0, 2), (1, 0), (2, 3), (3, 1))
GATHER_B = ((1, 2), (2, 1))
SCATTER_A = tuple((dst, src) for src, dst in GATHER_A)
SCATTER_B = GATHER_B


def ring(n, step):
    return [(i, (i + step) % n) for i in range(n)]


def params(mib=48):
    return pltpu.CompilerParams(vmem_limit_bytes=mib * 1024 * 1024)


def reach_kernel(ids_ref, bias_ref):
    groups = ids_ref.shape[0]
    row = lax.broadcasted_iota(jnp.int32, (GROUP, GROUP), 0)
    col = lax.broadcasted_iota(jnp.int32, (GROUP, GROUP), 1)
    base = jnp.where(col >= BLOCK, BLOCK, 0)
    inner = (col != 0) & (col != BLOCK)
    eye = row == col
    reach = []
    for g in range(groups):
        parent = ids_ref[g : g + 1, :] + base
        hit = ((parent == row) & inner) | eye
        reach.append(jnp.where(hit, 1.0, 0.0).astype(BF16))
    for sweep in range(6):
        reach = [
            jnp.minimum(jnp.dot(r, r, preferred_element_type=F32), 1.0).astype(BF16) for r in reach
        ]
    for g in range(groups):
        bias = jnp.where(reach[g].astype(F32) > 0.0, 0.0, -1e30)
        bias_ref[g * GROUP : (g + 1) * GROUP, :] = bias.T


def reach_bias(ids):
    groups = ids.shape[0]
    return pl.pallas_call(
        reach_kernel,
        out_shape=jax.ShapeDtypeStruct((groups * GROUP, GROUP), F32),
        compiler_params=params(16),
        cost_estimate=pl.CostEstimate(
            flops=groups * 6 * 2 * GROUP**3, bytes_accessed=groups * GROUP * GROUP * 4, transcendentals=0
        ),
        name="reach",
    )(ids)


def attention_kernel(width, x_ref, sq_ref, bias_ref, gain_ref, sharp_ref, out_ref):
    groups = x_ref.shape[0] // GROUP
    heads = x_ref.shape[1] // HEAD
    row = lax.broadcasted_iota(jnp.int32, (GROUP, GROUP), 0)
    col = lax.broadcasted_iota(jnp.int32, (GROUP, GROUP), 1)
    eye = row == col
    gain = gain_ref[...]
    ones = jnp.ones((GROUP, HEAD), BF16)
    where = [
        (slice(g * GROUP, (g + 1) * GROUP), slice(h * HEAD, (h + 1) * HEAD), h)
        for g in range(groups)
        for h in range(heads)
    ]
    feats = []
    for g in range(groups):
        rows = slice(g * GROUP, (g + 1) * GROUP)
        scale = lax.rsqrt(sq_ref[0, g : g + 1, :] * (1.0 / width) + EPS)
        scale = jnp.sum(jnp.where(eye, scale, 0.0), axis=1, keepdims=True)
        normed = (x_ref[rows, :].astype(F32) * scale * gain).astype(BF16)
        feats += [normed[:, h * HEAD : (h + 1) * HEAD] for h in range(heads)]
    factor = math.log2(math.e) / math.sqrt(HEAD)
    scores = [
        lax.dot_general(f, f, (((1,), (1,)), ((), ())), preferred_element_type=F32) for f in feats
    ]
    scores = [
        s * (sharp_ref[0, h] * factor) + bias_ref[rows, :] for s, (rows, _, h) in zip(scores, where)
    ]
    tops = [jnp.max(s, axis=1, keepdims=True) for s in scores]
    terms = [jnp.exp2(s - top).astype(BF16) for s, top in zip(scores, tops)]
    sums = [
        jnp.dot(t, jnp.concatenate([f, ones], axis=1), preferred_element_type=F32)
        for t, f in zip(terms, feats)
    ]
    for value, (rows, cols, _) in zip(sums, where):
        out_ref[rows, cols] = (value[:, :HEAD] / value[:, HEAD:]).astype(BF16)


def attention(states, squares, bias, gain, sharp, width, start, rows):
    cols = states.shape[1]
    tile = min(rows, 256)
    first = start // tile
    sub = tile // GROUP
    return pl.pallas_call(
        functools.partial(attention_kernel, width),
        grid=(rows // tile,),
        in_specs=[
            pl.BlockSpec((tile, cols), lambda i: (first + i, 0)),
            pl.BlockSpec((1, sub, GROUP), lambda i: (first + i, 0, 0)),
            pl.BlockSpec((tile, GROUP), lambda i: (first + i, 0)),
            pl.BlockSpec((1, cols), lambda i: (0, 0)),
            pl.BlockSpec(memory_space=pltpu.SMEM),
        ],
        out_specs=pl.BlockSpec((tile, cols), lambda i: (i, 0)),
        out_shape=jax.ShapeDtypeStruct((rows, cols), BF16),
        compiler_params=params(16),
        cost_estimate=pl.CostEstimate(
            flops=rows * GROUP * cols * 16, bytes_accessed=rows * cols * 4, transcendentals=rows * GROUP * 4
        ),
        name="attention",
    )(states, squares.reshape(-1, sub, GROUP), bias, gain, sharp)


def vmem():
    return pl.BlockSpec(memory_space=pltpu.VMEM)


def smem():
    return pl.BlockSpec(memory_space=pltpu.SMEM)


def hbm():
    return pl.BlockSpec(memory_space=pltpu.MemorySpace.HBM)


def forward_kernel(pos_ref, *refs):
    *mixed_refs, weight_ref, keep_ref, send_ref, mixed, weight, sems = refs
    loads = []
    for b, ref in enumerate(mixed_refs):
        pair = (
            pltpu.make_async_copy(ref, mixed.at[b], sems.at[0, b]),
            pltpu.make_async_copy(weight_ref.at[pos_ref[1 + b]], weight.at[b], sems.at[1, b]),
        )
        for load in pair:
            load.start()
        loads.append(pair)
    total = None
    for b, pair in enumerate(loads):
        for load in pair:
            load.wait()
        term = jnp.dot(mixed[b], weight[b], preferred_element_type=F32)
        total = term if total is None else total + term
    half = keep_ref.shape[1]
    send_ref[...] = total[:, half:].astype(BF16)
    keep_ref[...] = total[:, :half]


def forward(pos, mixed, weight):
    blocks, depth, cols = weight.shape
    cols = cols // 2
    rows = mixed[0].shape[0]
    return pl.pallas_call(
        forward_kernel,
        in_specs=[smem()] + [hbm()] * (len(mixed) + 1),
        out_specs=[vmem()] * 2,
        out_shape=[
            jax.ShapeDtypeStruct((rows, cols), F32),
            jax.ShapeDtypeStruct((rows, cols), BF16),
        ],
        scratch_shapes=[
            pltpu.VMEM((blocks, rows, depth), BF16),
            pltpu.VMEM(weight.shape, BF16),
            pltpu.SemaphoreType.DMA((2, blocks)),
        ],
        compiler_params=params(60),
        cost_estimate=pl.CostEstimate(
            flops=4 * rows * blocks * depth * cols,
            bytes_accessed=2 * rows * blocks * depth + 4 * blocks * depth * cols,
            transcendentals=0,
        ),
        name="forward",
    )(pos, *mixed, weight)


def residual_kernel(keep_ref, got_ref, target_ref, predicted_ref, grad_ref):
    result = keep_ref[...] + got_ref[...].astype(F32)
    predicted_ref[...] = result.astype(BF16)
    grad_ref[...] = jnp.clip(result - target_ref[...].astype(F32), -1.0, 1.0).astype(BF16)


def residual(keep, got, future, start):
    rows, cols = keep.shape
    tile = min(rows, 256)
    here = pl.BlockSpec((tile, cols), lambda i: (i, 0))
    return pl.pallas_call(
        residual_kernel,
        grid=(rows // tile,),
        in_specs=[here, here, pl.BlockSpec((tile, cols), lambda i: (start // tile + i, 0))],
        out_specs=[here, here],
        out_shape=[jax.ShapeDtypeStruct((rows, cols), BF16)] * 2,
        compiler_params=params(8),
        cost_estimate=pl.CostEstimate(
            flops=4 * rows * cols, bytes_accessed=12 * rows * cols, transcendentals=0
        ),
        name="residual",
    )(keep, got, future)


def gradient_kernel(chunks, blocks, has_acc, pos_ref, *refs):
    refs = list(refs)
    sources = [refs[n * blocks : (n + 1) * blocks] for n in range(chunks)]
    refs = refs[chunks * blocks :]
    grads, refs = refs[: 2 * chunks], refs[2 * chunks :]
    acc_ref = refs.pop(0) if has_acc else None
    out_ref, *mixed = refs[: 1 + chunks]
    refs = refs[1 + chunks :]
    acc = refs.pop(0) if has_acc else None
    out, sems = refs
    size = out.shape[1]

    def place(ref, b):
        return ref.at[pl.ds(pl.multiple_of(pos_ref[1 + b] * size, size), size)]

    loads = []
    for b in range(blocks):
        step = [
            pltpu.make_async_copy(sources[n][b], mixed[n].at[b], sems.at[n, b])
            for n in range(chunks)
        ]
        if has_acc:
            step.append(
                pltpu.make_async_copy(place(acc_ref, b), acc.at[b], sems.at[chunks, b])
            )
        for load in step:
            load.start()
        loads.append(step)
    grads = [g[...].astype(F32).T.astype(BF16) for g in grads]
    first = pos_ref[0] * (size // 2)
    halves = ((first, grads[:chunks]), (size // 2 - first, grads[chunks:]))
    stores = []
    for b in range(blocks):
        for load in loads[b]:
            load.wait()
        for start, grad in halves:
            rows = pl.ds(pl.multiple_of(start, size // 2), size // 2)
            value = acc[b, rows, :] if has_acc else None
            for n in range(chunks):
                term = jnp.dot(grad[n], mixed[n][b], preferred_element_type=F32)
                value = term if value is None else value + term
            out[b, rows, :] = value.astype(out.dtype)
        store = pltpu.make_async_copy(out.at[b], place(out_ref, b), sems.at[chunks + 1, b])
        store.start()
        stores.append(store)
    for store in stores:
        store.wait()


def gradient(pos, mixed, mine, other, acc, dtype):
    chunks = len(mixed)
    blocks = len(mixed[0])
    rows = [m[0].shape[0] for m in mixed]
    depth = mixed[0][0].shape[1]
    half = mine[0].shape[1]
    shape = (blocks, 2 * half, depth)
    operands = [*(value for chunk in mixed for value in chunk), *mine, *other]
    in_specs = [smem()] + [hbm()] * (chunks * blocks) + [vmem()] * (2 * chunks)
    scratch = [pltpu.VMEM((blocks, count, depth), BF16) for count in rows]
    if acc is not None:
        operands.append(acc)
        in_specs.append(hbm())
        scratch.append(pltpu.VMEM(shape, F32))
    scratch += [pltpu.VMEM(shape, dtype), pltpu.SemaphoreType.DMA((chunks + 2, blocks))]
    return pl.pallas_call(
        functools.partial(gradient_kernel, chunks, blocks, acc is not None),
        in_specs=in_specs,
        out_specs=hbm(),
        out_shape=jax.ShapeDtypeStruct((blocks * 2 * half, depth), dtype),
        scratch_shapes=scratch,
        compiler_params=params(60),
        cost_estimate=pl.CostEstimate(
            flops=4 * sum(rows) * blocks * depth * half,
            bytes_accessed=2 * sum(rows) * blocks * depth + 8 * blocks * depth * half,
            transcendentals=0,
        ),
        name="gradient",
    )(pos, *operands)


def after(value, *others):
    return lax.optimization_barrier((value, *others))[0]


def swap(value, axis):
    return lax.ppermute(value, axis, ring(2, 1))


def body(states, gain, sharpness, ancestor_ids, proposal, future):
    tokens, width = states.shape
    total_width = gain.shape[0]
    xh, xl = lax.axis_index("xh"), lax.axis_index("xl")
    y, c = lax.axis_index("y"), lax.axis_index("c")
    heads = width // HEAD

    order = [2 * ((y + dy) & 3) + (c ^ dc) for dc in (0, 1) for dy in (0, 3, 1, 2)]
    pos = jnp.stack([1 - (xl ^ xh), *order]).astype(jnp.int32)
    place = 8 * xl + 2 * y + c
    my_gain = lax.dynamic_slice_in_dim(gain, place * width, width).reshape(1, width)
    my_sharp = lax.dynamic_slice_in_dim(sharpness, place * heads, heads).reshape(1, heads)
    bias = reach_bias(ancestor_ids.reshape(-1, GROUP))

    first = lax.ppermute(proposal, ("xh", "xl"), GATHER_A)
    second = lax.ppermute(proposal, ("xh", "xl"), GATHER_B)
    wide = states.astype(F32)
    squares = jnp.sum(wide * wide, axis=1).reshape(-1, GROUP)
    squares = squares + swap(squares, "c")
    there = swap(squares, "xl")
    there, bias, my_gain, my_sharp = lax.optimization_barrier((there, bias, my_gain, my_sharp))
    squares = squares + there
    first, second, squares = lax.optimization_barrier((first, second, squares))
    kept = jnp.where(xh == xl, proposal, first)
    sent = jnp.where(xh == xl, first, second)
    weight = lax.all_gather(jnp.concatenate([kept, sent], axis=1), "z", axis=0, tiled=False)
    squares = squares + sum(lax.ppermute(squares, "y", ring(4, k)) for k in (1, 2, 3))

    count = len(CHUNKS)
    starts = [sum(CHUNKS[:i]) for i in range(count)]
    made, mixed, up, down, far = [], [], [], [], []
    for i, (start, rows) in enumerate(zip(starts, CHUNKS)):
        if i >= 1:
            squares = after(squares, mixed[0], *up[: min(i - 1, 1)])
        source = attention(states, squares, bias, my_gain, my_sharp, total_width, start, rows)
        made.append(source)
        if i >= 2:
            source = after(source, up[i - 2], down[i - 2])
        mixed.append(source)
        up.append(lax.ppermute(source, "y", ring(4, 1)))
        down.append(lax.ppermute(source, "y", ring(4, -1)))

    def relay(i, *others):
        source, step = (up[i], 1) if FAR[i] else (down[i], -1)
        far.append(lax.ppermute(after(source, *others), "y", ring(4, step)))

    def blocks(i, *others):
        here = (mixed[i], up[i], down[i], far[i])
        return [*here, *(swap(after(value, *others), "c") for value in here)]

    def multiply(i):
        kept, sent = forward(pos, full[i], weight)
        keep.append(kept)
        send.append(sent)
        got.append(swap(sent, "xl"))

    def receive(i, *others):
        value, grad = residual(after(keep[i], *others), got[i], future, starts[i])
        predicted.append(value)
        mine.append(grad)
        other.append(swap(mine[i], "xl"))

    predicted, full, keep, send, got, mine, other = [], [], [], [], [], [], []
    relay(0, *made[2:])
    relay(1)
    full.append(blocks(0))
    full.append(blocks(1))
    relay(2)
    relay(3)
    full[0][0] = after(full[0][0], up[2], down[2])
    multiply(0)
    full[1][0] = after(full[1][0], send[0], up[3], down[3])
    multiply(1)
    full.append(blocks(2, send[1]))
    receive(0, send[1])
    receive(1)
    full[2][0] = after(full[2][0], other[0], mine[1])
    multiply(2)
    full.append(blocks(3, send[1], mine[0]))
    full[3][0] = after(full[3][0], send[2], other[1])
    multiply(3)
    receive(2, send[3])
    receive(3, mine[2])
    acc = gradient(pos, full[:2], mine[:2], [after(other[0], mine[3]), other[1]], None, F32)
    acc = gradient(pos, full[2:], mine[2:], other[2:], acc, BF16)

    summed = lax.psum_scatter(acc, "z", scatter_dimension=0, tiled=True)
    to_a, to_b = jnp.split(summed, 2)
    got_a = lax.ppermute(to_a, ("xh", "xl"), SCATTER_A)
    got_b = lax.ppermute(to_b, ("xh", "xl"), SCATTER_B)
    got_b = jnp.where(xh == xl, to_b, got_b)
    weight_grad = (got_a.astype(F32) + got_b.astype(F32)).T / math.sqrt(
        tokens * lax.axis_size("xh") * lax.axis_size("z")
    )
    return jnp.concatenate(predicted), weight_grad


def solution(mesh):
    grid = Mesh(mesh.devices.reshape(2, 8, 2, 4, 2), ("xh", "z", "xl", "y", "c"))
    dp, tensor = ("xh", "z"), ("xl", "y", "c")
    return jax.shard_map(
        body,
        mesh=grid,
        in_specs=(P(dp, tensor), P(), P(), P(dp), P(dp, tensor), P(dp, tensor)),
        out_specs=(P(dp, tensor), P(dp, tensor)),
        check_vma=False,
    )
```

```python
import functools
import math

import jax
import jax.numpy as jnp
from jax import lax
from jax.experimental import pallas as pl
from jax.experimental.pallas import tpu as pltpu
from jax.sharding import Mesh
from jax.sharding import PartitionSpec as P

HEAD = 128
BLOCK = 64
GROUP = 128
EPS = 1e-05
CHUNKS = (768, 512, 512, 256)
FAR = (True, False, False, True)
BF16 = jnp.bfloat16
F32 = jnp.float32

GATHER_A = ((0, 2), (1, 0), (2, 3), (3, 1))
GATHER_B = ((1, 2), (2, 1))
SCATTER_A = tuple((dst, src) for src, dst in GATHER_A)
SCATTER_B = GATHER_B


def ring(n, step):
    return [(i, (i + step) % n) for i in range(n)]


def params(mib=48):
    return pltpu.CompilerParams(vmem_limit_bytes=mib * 1024 * 1024)


def reach_kernel(ids_ref, bias_ref):
    groups = ids_ref.shape[0]
    row = lax.broadcasted_iota(jnp.int32, (GROUP, GROUP), 0)
    col = lax.broadcasted_iota(jnp.int32, (GROUP, GROUP), 1)
    base = jnp.where(col >= BLOCK, BLOCK, 0)
    inner = (col != 0) & (col != BLOCK)
    eye = row == col
    reach = []
    for g in range(groups):
        parent = ids_ref[g : g + 1, :] + base
        hit = ((parent == row) & inner) | eye
        reach.append(jnp.where(hit, 1.0, 0.0).astype(BF16))
    for sweep in range(6):
        reach = [
            jnp.minimum(jnp.dot(r, r, preferred_element_type=F32), 1.0).astype(BF16) for r in reach
        ]
    for g in range(groups):
        bias = jnp.where(reach[g].astype(F32) > 0.0, 0.0, -1e30)
        bias_ref[g * GROUP : (g + 1) * GROUP, :] = bias.T


def reach_bias(ids):
    groups = ids.shape[0]
    return pl.pallas_call(
        reach_kernel,
        out_shape=jax.ShapeDtypeStruct((groups * GROUP, GROUP), F32),
        compiler_params=params(16),
        cost_estimate=pl.CostEstimate(
            flops=groups * 6 * 2 * GROUP**3, bytes_accessed=groups * GROUP * GROUP * 4, transcendentals=0
        ),
        name="reach",
    )(ids)


def attention_kernel(width, x_ref, sq_ref, bias_ref, gain_ref, sharp_ref, out_ref):
    groups = x_ref.shape[0] // GROUP
    heads = x_ref.shape[1] // HEAD
    row = lax.broadcasted_iota(jnp.int32, (GROUP, GROUP), 0)
    col = lax.broadcasted_iota(jnp.int32, (GROUP, GROUP), 1)
    eye = row == col
    gain = gain_ref[...]
    ones = jnp.ones((GROUP, HEAD), BF16)
    where = [
        (slice(g * GROUP, (g + 1) * GROUP), slice(h * HEAD, (h + 1) * HEAD), h)
        for g in range(groups)
        for h in range(heads)
    ]
    feats = []
    for g in range(groups):
        rows = slice(g * GROUP, (g + 1) * GROUP)
        scale = lax.rsqrt(sq_ref[0, g : g + 1, :] * (1.0 / width) + EPS)
        scale = jnp.sum(jnp.where(eye, scale, 0.0), axis=1, keepdims=True)
        normed = (x_ref[rows, :].astype(F32) * scale * gain).astype(BF16)
        feats += [normed[:, h * HEAD : (h + 1) * HEAD] for h in range(heads)]
    factor = math.log2(math.e) / math.sqrt(HEAD)
    scores = [
        lax.dot_general(f, f, (((1,), (1,)), ((), ())), preferred_element_type=F32) for f in feats
    ]
    scores = [
        s * (sharp_ref[0, h] * factor) + bias_ref[rows, :] for s, (rows, _, h) in zip(scores, where)
    ]
    tops = [jnp.max(s, axis=1, keepdims=True) for s in scores]
    terms = [jnp.exp2(s - top).astype(BF16) for s, top in zip(scores, tops)]
    sums = [
        jnp.dot(t, jnp.concatenate([f, ones], axis=1), preferred_element_type=F32)
        for t, f in zip(terms, feats)
    ]
    for value, (rows, cols, _) in zip(sums, where):
        out_ref[rows, cols] = (value[:, :HEAD] / value[:, HEAD:]).astype(BF16)


def attention(states, squares, bias, gain, sharp, width, start, rows):
    cols = states.shape[1]
    tile = min(rows, 256)
    first = start // tile
    sub = tile // GROUP
    return pl.pallas_call(
        functools.partial(attention_kernel, width),
        grid=(rows // tile,),
        in_specs=[
            pl.BlockSpec((tile, cols), lambda i: (first + i, 0)),
            pl.BlockSpec((1, sub, GROUP), lambda i: (first + i, 0, 0)),
            pl.BlockSpec((tile, GROUP), lambda i: (first + i, 0)),
            pl.BlockSpec((1, cols), lambda i: (0, 0)),
            pl.BlockSpec(memory_space=pltpu.SMEM),
        ],
        out_specs=pl.BlockSpec((tile, cols), lambda i: (i, 0)),
        out_shape=jax.ShapeDtypeStruct((rows, cols), BF16),
        compiler_params=params(16),
        cost_estimate=pl.CostEstimate(
            flops=rows * GROUP * cols * 16, bytes_accessed=rows * cols * 4, transcendentals=rows * GROUP * 4
        ),
        name="attention",
    )(states, squares.reshape(-1, sub, GROUP), bias, gain, sharp)


def vmem():
    return pl.BlockSpec(memory_space=pltpu.VMEM)


def smem():
    return pl.BlockSpec(memory_space=pltpu.SMEM)


def hbm():
    return pl.BlockSpec(memory_space=pltpu.MemorySpace.HBM)


def forward_kernel(pos_ref, *refs):
    *mixed_refs, weight_ref, keep_ref, send_ref, mixed, weight, sems = refs
    loads = []
    for b, ref in enumerate(mixed_refs):
        pair = (
            pltpu.make_async_copy(ref, mixed.at[b], sems.at[0, b]),
            pltpu.make_async_copy(weight_ref.at[pos_ref[1 + b]], weight.at[b], sems.at[1, b]),
        )
        for load in pair:
            load.start()
        loads.append(pair)
    total = None
    for b, pair in enumerate(loads):
        for load in pair:
            load.wait()
        term = jnp.dot(mixed[b], weight[b], preferred_element_type=F32)
        total = term if total is None else total + term
    half = keep_ref.shape[1]
    send_ref[...] = total[:, half:].astype(BF16)
    keep_ref[...] = total[:, :half]


def forward(pos, mixed, weight):
    blocks, depth, cols = weight.shape
    cols = cols // 2
    rows = mixed[0].shape[0]
    return pl.pallas_call(
        forward_kernel,
        in_specs=[smem()] + [hbm()] * (len(mixed) + 1),
        out_specs=[vmem()] * 2,
        out_shape=[
            jax.ShapeDtypeStruct((rows, cols), F32),
            jax.ShapeDtypeStruct((rows, cols), BF16),
        ],
        scratch_shapes=[
            pltpu.VMEM((blocks, rows, depth), BF16),
            pltpu.VMEM(weight.shape, BF16),
            pltpu.SemaphoreType.DMA((2, blocks)),
        ],
        compiler_params=params(60),
        cost_estimate=pl.CostEstimate(
            flops=4 * rows * blocks * depth * cols,
            bytes_accessed=2 * rows * blocks * depth + 4 * blocks * depth * cols,
            transcendentals=0,
        ),
        name="forward",
    )(pos, *mixed, weight)


def residual_kernel(keep_ref, got_ref, target_ref, predicted_ref, grad_ref):
    result = keep_ref[...] + got_ref[...].astype(F32)
    predicted_ref[...] = result.astype(BF16)
    grad_ref[...] = jnp.clip(result - target_ref[...].astype(F32), -1.0, 1.0).astype(BF16)


def residual(keep, got, future, start):
    rows, cols = keep.shape
    tile = min(rows, 256)
    here = pl.BlockSpec((tile, cols), lambda i: (i, 0))
    return pl.pallas_call(
        residual_kernel,
        grid=(rows // tile,),
        in_specs=[here, here, pl.BlockSpec((tile, cols), lambda i: (start // tile + i, 0))],
        out_specs=[here, here],
        out_shape=[jax.ShapeDtypeStruct((rows, cols), BF16)] * 2,
        compiler_params=params(8),
        cost_estimate=pl.CostEstimate(
            flops=4 * rows * cols, bytes_accessed=12 * rows * cols, transcendentals=0
        ),
        name="residual",
    )(keep, got, future)


def gradient_kernel(chunks, blocks, has_acc, pos_ref, *refs):
    refs = list(refs)
    sources = [refs[n * blocks : (n + 1) * blocks] for n in range(chunks)]
    refs = refs[chunks * blocks :]
    grads, refs = refs[: 2 * chunks], refs[2 * chunks :]
    acc_ref = refs.pop(0) if has_acc else None
    out_ref, *mixed = refs[: 1 + chunks]
    refs = refs[1 + chunks :]
    acc = refs.pop(0) if has_acc else None
    out, sems = refs
    size = out.shape[1]

    def place(ref, b):
        return ref.at[pl.ds(pl.multiple_of(pos_ref[1 + b] * size, size), size)]

    loads = []
    for b in range(blocks):
        step = [
            pltpu.make_async_copy(sources[n][b], mixed[n].at[b], sems.at[n, b])
            for n in range(chunks)
        ]
        if has_acc:
            step.append(
                pltpu.make_async_copy(place(acc_ref, b), acc.at[b], sems.at[chunks, b])
            )
        for load in step:
            load.start()
        loads.append(step)
    grads = [g[...].astype(F32).T.astype(BF16) for g in grads]
    first = pos_ref[0] * (size // 2)
    halves = ((first, grads[:chunks]), (size // 2 - first, grads[chunks:]))
    stores = []
    for b in range(blocks):
        for load in loads[b]:
            load.wait()
        for start, grad in halves:
            rows = pl.ds(pl.multiple_of(start, size // 2), size // 2)
            value = acc[b, rows, :] if has_acc else None
            for n in range(chunks):
                term = jnp.dot(grad[n], mixed[n][b], preferred_element_type=F32)
                value = term if value is None else value + term
            out[b, rows, :] = value.astype(out.dtype)
        store = pltpu.make_async_copy(out.at[b], place(out_ref, b), sems.at[chunks + 1, b])
        store.start()
        stores.append(store)
    for store in stores:
        store.wait()


def gradient(pos, mixed, mine, other, acc, dtype):
    chunks = len(mixed)
    blocks = len(mixed[0])
    rows = [m[0].shape[0] for m in mixed]
    depth = mixed[0][0].shape[1]
    half = mine[0].shape[1]
    shape = (blocks, 2 * half, depth)
    operands = [*(value for chunk in mixed for value in chunk), *mine, *other]
    in_specs = [smem()] + [hbm()] * (chunks * blocks) + [vmem()] * (2 * chunks)
    scratch = [pltpu.VMEM((blocks, count, depth), BF16) for count in rows]
    if acc is not None:
        operands.append(acc)
        in_specs.append(hbm())
        scratch.append(pltpu.VMEM(shape, F32))
    scratch += [pltpu.VMEM(shape, dtype), pltpu.SemaphoreType.DMA((chunks + 2, blocks))]
    return pl.pallas_call(
        functools.partial(gradient_kernel, chunks, blocks, acc is not None),
        in_specs=in_specs,
        out_specs=hbm(),
        out_shape=jax.ShapeDtypeStruct((blocks * 2 * half, depth), dtype),
        scratch_shapes=scratch,
        compiler_params=params(60),
        cost_estimate=pl.CostEstimate(
            flops=4 * sum(rows) * blocks * depth * half,
            bytes_accessed=2 * sum(rows) * blocks * depth + 8 * blocks * depth * half,
            transcendentals=0,
        ),
        name="gradient",
    )(pos, *operands)


def after(value, *others):
    return lax.optimization_barrier((value, *others))[0]


def swap(value, axis):
    return lax.ppermute(value, axis, ring(2, 1))


def body(states, gain, sharpness, ancestor_ids, proposal, future):
    tokens, width = states.shape
    total_width = gain.shape[0]
    xh, xl = lax.axis_index("xh"), lax.axis_index("xl")
    y, c = lax.axis_index("y"), lax.axis_index("c")
    heads = width // HEAD

    order = [2 * ((y + dy) & 3) + (c ^ dc) for dc in (0, 1) for dy in (0, 3, 1, 2)]
    pos = jnp.stack([1 - (xl ^ xh), *order]).astype(jnp.int32)
    place = 8 * xl + 2 * y + c
    my_gain = lax.dynamic_slice_in_dim(gain, place * width, width).reshape(1, width)
    my_sharp = lax.dynamic_slice_in_dim(sharpness, place * heads, heads).reshape(1, heads)
    bias = reach_bias(ancestor_ids.reshape(-1, GROUP))

    first = lax.ppermute(proposal, ("xh", "xl"), GATHER_A)
    second = lax.ppermute(proposal, ("xh", "xl"), GATHER_B)
    wide = states.astype(F32)
    squares = jnp.sum(wide * wide, axis=1).reshape(-1, GROUP)
    squares = squares + swap(squares, "c")
    there = swap(squares, "xl")
    there, bias, my_gain, my_sharp = lax.optimization_barrier((there, bias, my_gain, my_sharp))
    squares = squares + there
    first, second, squares = lax.optimization_barrier((first, second, squares))
    kept = jnp.where(xh == xl, proposal, first)
    sent = jnp.where(xh == xl, first, second)
    weight = lax.all_gather(jnp.concatenate([kept, sent], axis=1), "z", axis=0, tiled=False)
    squares = squares + sum(lax.ppermute(squares, "y", ring(4, k)) for k in (1, 2, 3))

    count = len(CHUNKS)
    starts = [sum(CHUNKS[:i]) for i in range(count)]
    made, mixed, up, down, far = [], [], [], [], []
    for i, (start, rows) in enumerate(zip(starts, CHUNKS)):
        if i >= 1:
            squares = after(squares, mixed[0], *up[: min(i - 1, 1)])
        source = attention(states, squares, bias, my_gain, my_sharp, total_width, start, rows)
        made.append(source)
        if i >= 2:
            source = after(source, up[i - 2], down[i - 2])
        mixed.append(source)
        up.append(lax.ppermute(source, "y", ring(4, 1)))
        down.append(lax.ppermute(source, "y", ring(4, -1)))

    def relay(i, *others):
        source, step = (up[i], 1) if FAR[i] else (down[i], -1)
        far.append(lax.ppermute(after(source, *others), "y", ring(4, step)))

    def blocks(i, *others):
        here = (mixed[i], up[i], down[i], far[i])
        return [*here, *(swap(after(value, *others), "c") for value in here)]

    def multiply(i):
        kept, sent = forward(pos, full[i], weight)
        keep.append(kept)
        send.append(sent)
        got.append(swap(sent, "xl"))

    def receive(i, *others):
        value, grad = residual(after(keep[i], *others), got[i], future, starts[i])
        predicted.append(value)
        mine.append(grad)
        other.append(swap(mine[i], "xl"))

    predicted, full, keep, send, got, mine, other = [], [], [], [], [], [], []
    relay(0, *made[2:])
    relay(1)
    full.append(blocks(0))
    full.append(blocks(1))
    relay(2)
    relay(3)
    full[0][0] = after(full[0][0], up[2], down[2])
    multiply(0)
    full[1][0] = after(full[1][0], send[0], up[3], down[3])
    multiply(1)
    full.append(blocks(2, send[1]))
    receive(0, send[1])
    receive(1)
    full[2][0] = after(full[2][0], other[0], mine[1])
    multiply(2)
    full.append(blocks(3, send[1], mine[0]))
    full[3][0] = after(full[3][0], send[2], other[1])
    multiply(3)
    receive(2, send[3])
    acc = gradient(pos, full[:2], mine[:2], [other[0], after(other[1], mine[2])], None, F32)
    receive(3, acc)
    acc = gradient(pos, full[2:], mine[2:], other[2:], acc, BF16)

    summed = lax.psum_scatter(acc, "z", scatter_dimension=0, tiled=True)
    to_a, to_b = jnp.split(summed, 2)
    got_a = lax.ppermute(to_a, ("xh", "xl"), SCATTER_A)
    got_b = lax.ppermute(to_b, ("xh", "xl"), SCATTER_B)
    got_b = jnp.where(xh == xl, to_b, got_b)
    weight_grad = (got_a.astype(F32) + got_b.astype(F32)).T / math.sqrt(
        tokens * lax.axis_size("xh") * lax.axis_size("z")
    )
    return jnp.concatenate(predicted), weight_grad


def solution(mesh):
    grid = Mesh(mesh.devices.reshape(2, 8, 2, 4, 2), ("xh", "z", "xl", "y", "c"))
    dp, tensor = ("xh", "z"), ("xl", "y", "c")
    return jax.shard_map(
        body,
        mesh=grid,
        in_specs=(P(dp, tensor), P(), P(), P(dp), P(dp, tensor), P(dp, tensor)),
        out_specs=(P(dp, tensor), P(dp, tensor)),
        check_vma=False,
    )
```
